512 devices in a mesh: dp: 64 (over x, y_hi, z), tensor: 8 (over y_lo, core).
Axes of the slice: x: 4, y: 8 (y_hi: 2, y_lo: 4; y = y_hi * 4 + y_lo), z: 8, core: 2. Of those that a mesh axis runs over, the one named last changes fastest.
Arguments:
- query_inputs: bfloat16 [4, 256, 32, 8192], P(None, 'dp', None, 'tensor'), may hold values from -6 to 6
- query_output_grads: bfloat16 [4, 256, 32, 8192], P(None, 'dp', None, 'tensor'), may hold values from -6 to 6
- in_projection: bfloat16 [4, 64, 8192], P(None, None, 'tensor'), may hold values from -0.0625 to 0.0625
- out_projection: bfloat16 [4, 64, 8192], P(None, None, 'tensor'), may hold values from -0.0625 to 0.0625
- train_grads: bfloat16 [16384, 16384], P(('dp', 'tensor')), may hold values from -0.01171875 to 0.01171875
- lengths: int32 [256], P('dp'), may hold values from 1 to 32
- loss_mask: int32 [256, 32], P('dp'), may hold values 0 or 1
- domains: int32 [256, 1], replicated, may hold values from 0 to 7
Outputs:
- scores: float32 [16384, 256], P(('dp', 'tensor'))
- domain_influence: float32 [16384, 8], P(('dp', 'tensor'))
The draws below stay inside these ranges and needn't reach their ends.
Inputs may be any that keep to these rules, and one draw needn't show every extreme that they name: `domains`: every domain has at least one query example.
All inputs are finite; a program needn't handle non-finite values. No bound on the sum of `loss_mask` on one device may be relied on, other than what follows from the above.
Results may differ from the reference program's by a relative error of at most 0.0029.
Values may be sent and summed in bfloat16 or wider, within the bound.
No kernel may reach another device: no remote copies, remote signals or barrier semaphores. Data moves between devices by JAX's collectives and lax.ppermute only.
A program may use at most 64 MiB of HBM per device.

```python
import jax
import jax.numpy as jnp
from jax import lax

D = 8192
K_IN = 64
K_OUT = 64
LAYERS = 4
SEQ = 32
DOMAINS = 8
R_DEV = 32
KTOT = 16384
QUERIES = 256
TRAIN = 16384
N_DP = 64
N_TENSOR = 8


def touch_ends(values, stream_key, least, largest):
    shape = values.shape
    place = [jax.random.randint(jax.random.fold_in(stream_key, axis), (), 0, shape[axis]) for axis in range(len(shape))]
    values = values.at[tuple(place)].set(least)
    longest = shape.index(max(shape))
    place[longest] = (place[longest] + 1) % shape[longest]
    return values.at[tuple(place)].set(largest)


def block_levels(rng, extent, pieces, smallest, top_value):
    gain = 1.0
    for axis_at, blocks in pieces:
        draws = jax.random.uniform(jax.random.fold_in(jax.random.fold_in(rng, 6), axis_at), (blocks,), jnp.float32, smallest / len(pieces), top_value / len(pieces))
        gain = gain * jnp.repeat(jnp.exp(draws), extent[axis_at] // blocks).reshape((-1,) + (1,) * (len(extent) - 1 - axis_at))
    return gain


def choose_distinct(key, rows, count, top, lift):
    order = jax.random.permutation(jax.random.fold_in(key, 1), count)
    boost = order
    for power in range(3):
        boost = boost * boost // count
    boost = boost * lift // count
    tickets = jax.random.randint(jax.random.fold_in(key, 2), (rows, count), 0, 4096) + boost
    fixed_rows = jax.random.permutation(jax.random.fold_in(key, 3), rows)[jnp.arange(count) % rows]
    tickets = jnp.where(jnp.arange(rows)[:, None] == fixed_rows[None, :], 1 << 14, tickets)
    merit = tickets * count + jnp.arange(count)
    return lax.top_k(merit.astype(jnp.int32), top)[1].astype(jnp.int32)


def bell_draw(stream_key, extent, deviation, reach, pieces=(), kind=jnp.bfloat16):
    drawn = deviation * jax.random.normal(stream_key, extent, jnp.float32)
    if pieces:
        drawn = drawn * block_levels(stream_key, extent, pieces, -0.22, 0.18)
    return jnp.clip(drawn, -reach, reach).astype(kind)


def setup_inputs(seed: int = 0) -> dict:
    key_of = jax.random.split(jax.random.key(seed), 9)
    query_inputs = bell_draw(key_of[0], (LAYERS, QUERIES, SEQ, D), 1.0, 6.0, ((1, 64), (3, 8)))
    query_output_grads = bell_draw(key_of[1], (LAYERS, QUERIES, SEQ, D), 1.0, 6.0, ((1, 64), (3, 8)))
    in_projection = bell_draw(key_of[2], (LAYERS, K_IN, D), D ** -0.5, 0.0625, ((2, 8),))
    out_projection = bell_draw(key_of[3], (LAYERS, K_OUT, D), D ** -0.5, 0.0625, ((2, 8),))
    train_grads = bell_draw(key_of[4], (TRAIN, KTOT), (0.25 / (KTOT ** 0.5)), 0.01171875, ((0, 512),))
    lengths = touch_ends(jax.random.randint(key_of[5], (QUERIES,), 1, SEQ + 1), jax.random.fold_in(key_of[5], 1), 1, SEQ).astype(jnp.int32)
    loss_mask = touch_ends((jax.random.randint(key_of[6], (QUERIES, SEQ), 0, 4) < 3).astype(jnp.int32), jax.random.fold_in(key_of[6], 1), 0, 1)
    domains = choose_distinct(key_of[7], QUERIES, DOMAINS, 1, 1024)
    return dict(query_inputs=query_inputs, query_output_grads=query_output_grads, in_projection=in_projection, out_projection=out_projection, train_grads=train_grads, lengths=lengths, loss_mask=loss_mask, domains=domains)


def reference(query_inputs, query_output_grads, in_projection, out_projection, train_grads, lengths, loss_mask, domains):
    highest = lax.Precision.HIGHEST
    positions = lax.broadcasted_iota(jnp.int32, loss_mask.shape, 1)
    token_weight = jnp.where(positions < lengths[:, None], loss_mask, 0).astype(jnp.float32)
    layer_grads = []
    for layer_index in range(LAYERS):
        inputs = query_inputs[layer_index].astype(jnp.float32)
        outputs = query_output_grads[layer_index].astype(jnp.float32)
        in_factor = jnp.einsum("qsd,kd->qsk", inputs, in_projection[layer_index].astype(jnp.float32), precision=highest)
        out_factor = jnp.einsum("qsd,kd->qsk", outputs, out_projection[layer_index].astype(jnp.float32), precision=highest)
        weighted = out_factor * token_weight[:, :, None]
        outer = jnp.einsum("qso,qsi->qoi", weighted, in_factor, precision=highest)
        layer_grads.append(outer.reshape(QUERIES, K_OUT * K_IN))
    query_grads = jnp.concatenate(layer_grads, axis=1).astype(jnp.bfloat16)
    query_wide = query_grads.astype(jnp.float32)
    row_blocks = train_grads.reshape(N_DP, R_DEV * N_TENSOR, KTOT)

    def block_scores(row_block):
        return jnp.dot(row_block.astype(jnp.float32), query_wide.T, precision=highest)

    scores = lax.map(block_scores, row_blocks).reshape(TRAIN, QUERIES)
    onehot = (domains == lax.broadcasted_iota(jnp.int32, (1, DOMAINS), 1)).astype(jnp.float32)
    counts = jnp.sum(onehot, axis=0)
    domain_influence = jnp.dot(scores, onehot, precision=highest) / counts[None, :]
    return scores, domain_influence
```

```python
import functools

import jax
import jax.numpy as jnp
from jax import lax
from jax.experimental import pallas as pl
from jax.experimental.pallas import tpu as pltpu
from jax.sharding import PartitionSpec as P

LAYERS = 4
SEQ = 32
WIDTH = 64
DOMAINS = 8
AXES = ("dp", "tensor")
NX, NY, NZ, NC = 4, 8, 8, 2
LANES = 128
PAIRS = WIDTH * WIDTH // LANES


def flat(x, y, z, c):
    return (x * 16 + (y // 4) * 8 + z) * 8 + (y % 4) * 2 + c


def places():
    return [(x, y, z, c) for x in range(NX) for y in range(NY) for z in range(NZ) for c in range(NC)]


def partition(members):
    groups, seen = [], set()
    for place in places():
        group = [flat(*m) for m in members(*place)]
        if group[0] not in seen:
            seen.update(group)
            groups.append(group)
    return groups


def along_x(x, y, z, c):
    return [(i, y, z, c) for i in range(NX)]


def far_members(x, y, z, c):
    return [
        ((x & 1) | (xh << 1), (h << 2) | ((y & 3) ^ (((x >> 1) ^ xh) << 1)), (z & 1) | (zz << 1), c)
        for xh in range(2)
        for h in range(2)
        for zz in range(4)
    ]


def near_members(x, y, z, c):
    return [
        ((x & 2) | xl, y ^ ((x & 1) ^ xl), (z & 6) | zl, c)
        for xl in range(2)
        for zl in range(2)
    ]


def project_kernel(place_ref, in_ref, grad_ref, in_proj_ref, out_proj_ref, out_ref):
    def side(rows_ref, proj_ref):
        rows = rows_ref[0].reshape(-1, rows_ref.shape[-1])
        return lax.dot_general(
            rows, proj_ref[0], (((1,), (1,)), ((), ())), preferred_element_type=jnp.float32
        )

    out_ref[0] = jnp.concatenate([side(in_ref, in_proj_ref), side(grad_ref, out_proj_ref)], axis=1)


def project(place, query_inputs, query_output_grads, in_projection, out_projection):
    _, queries, seq, depth = query_inputs.shape
    rows = pl.BlockSpec((1, queries, seq, depth), lambda j, place: (place[0] ^ j, 0, 0, 0))
    proj = pl.BlockSpec((1, WIDTH, depth), lambda j, place: (place[0] ^ j, 0, 0))
    return pl.pallas_call(
        project_kernel,
        out_shape=jax.ShapeDtypeStruct((LAYERS, queries * seq, 2 * WIDTH), jnp.float32),
        grid_spec=pltpu.PrefetchScalarGridSpec(
            num_scalar_prefetch=1,
            grid=(LAYERS,),
            in_specs=[rows, rows, proj, proj],
            out_specs=pl.BlockSpec((1, queries * seq, 2 * WIDTH), lambda j, place: (j, 0, 0)),
        ),
        compiler_params=pltpu.CompilerParams(vmem_limit_bytes=16 * 1024 * 1024),
        name="project",
    )(place, query_inputs, query_output_grads, in_projection, out_projection)


def outer_kernel(place_ref, lengths_ref, mask_ref, parts_ref, out_ref, rows_ref):
    core = place_ref[1]
    total = parts_ref[0]
    for part in range(1, parts_ref.shape[0]):
        total = total + parts_ref[part]
    row = lax.broadcasted_iota(jnp.int32, (SEQ, SEQ), 0)
    col = lax.broadcasted_iota(jnp.int32, (SEQ, SEQ), 1)
    first = lax.broadcasted_iota(jnp.int32, (SEQ, LANES), 1) < WIDTH
    for k in range(2):
        mask = jnp.where(core == 0, mask_ref[k : k + 1, :], mask_ref[2 + k : 3 + k, :])
        kept = (row == col) & (col < lengths_ref[2 * core + k])
        weight = jnp.sum(jnp.where(kept, mask, 0).astype(jnp.float32), axis=1, keepdims=True)
        factors = total[k * SEQ : (k + 1) * SEQ]
        inner = factors[:, :WIDTH]
        inner = jnp.concatenate([inner, inner], axis=1)
        weighted = factors[:, WIDTH:] * weight
        for p in range(PAIRS):
            low = jnp.broadcast_to(weighted[:, 2 * p : 2 * p + 1], (SEQ, LANES))
            high = jnp.broadcast_to(weighted[:, 2 * p + 1 : 2 * p + 2], (SEQ, LANES))
            product = jnp.where(first, low, high) * inner
            rows_ref[2 * p + k : 2 * p + k + 1, :] = jnp.sum(product, axis=0, keepdims=True)
    out_ref[...] = rows_ref[...].astype(jnp.bfloat16)


def outer(place, lengths, loss_mask, parts):
    smem = pl.BlockSpec(memory_space=pltpu.SMEM)
    vmem = pl.BlockSpec(memory_space=pltpu.VMEM)
    return pl.pallas_call(
        outer_kernel,
        out_shape=jax.ShapeDtypeStruct((2 * PAIRS, LANES), jnp.bfloat16),
        in_specs=[smem, smem, vmem, vmem],
        out_specs=vmem,
        scratch_shapes=[pltpu.VMEM((2 * PAIRS, LANES), jnp.float32)],
        compiler_params=pltpu.CompilerParams(vmem_limit_bytes=16 * 1024 * 1024),
        name="outer",
    )(place, lengths, loss_mask, parts)


def finish_kernel(parts_ref, domains_ref, scores_ref, influence_ref):
    total = parts_ref[0]
    for part in range(1, parts_ref.shape[0]):
        total = total + parts_ref[part]
    queries = total.shape[1]
    here = lax.broadcasted_iota(jnp.int32, (queries, queries), 0)
    there = lax.broadcasted_iota(jnp.int32, (queries, queries), 1)

    def bit(value, at, to, bits=1):
        return ((value >> at) & ((1 << bits) - 1)) << to

    target = (
        bit(here, 7, 1) + bit(here, 6, 6) + bit(here, 5, 2) + bit(here, 4, 0) + bit(here, 3, 7)
        + bit(here, 2, 5) + bit(here, 0, 3, 2)
    )
    place = (target == there).astype(jnp.float32)
    scores = jnp.dot(total, place, precision=lax.Precision.HIGHEST, preferred_element_type=jnp.float32)
    scores_ref[...] = scores
    lane = lax.broadcasted_iota(jnp.int32, (queries, DOMAINS), 1)
    onehot = (domains_ref[...] == lane).astype(jnp.float32)
    counts = jnp.sum(onehot, axis=0, keepdims=True)
    sums = jnp.dot(scores, onehot, precision=lax.Precision.HIGHEST, preferred_element_type=jnp.float32)
    influence_ref[...] = sums / counts


def finish(parts, domains):
    _, rows, queries = parts.shape
    return pl.pallas_call(
        finish_kernel,
        out_shape=(
            jax.ShapeDtypeStruct((rows, queries), jnp.float32),
            jax.ShapeDtypeStruct((rows, DOMAINS), jnp.float32),
        ),
        compiler_params=pltpu.CompilerParams(vmem_limit_bytes=16 * 1024 * 1024),
        name="finish",
    )(parts, domains)


def score_kernel(place_ref, own_ref, first_ref, second_ref, third_ref, near_ref, mate_ref, out_ref, queries_ref):
    x, core = place_ref[0], place_ref[1]
    near, pairs, rows, lanes = near_ref.shape
    half = near * rows
    for block_ref, side in ((near_ref, core), (mate_ref, 1 - core)):
        for n in range(near):
            at = pl.ds(pl.multiple_of(side * half + n * rows, rows), rows)
            for p in range(pairs):
                queries_ref[at, p * lanes : (p + 1) * lanes] = block_ref[n, p]
    for step, rows_ref in enumerate((own_ref, first_ref, second_ref, third_ref)):
        out_ref[pl.ds(x ^ step, 1)] = lax.dot_general(
            rows_ref[...], queries_ref[...], (((1,), (1,)), ((), ())), preferred_element_type=jnp.float32
        )[None]


def score(place, blocks, near, mate):
    smem = pl.BlockSpec(memory_space=pltpu.SMEM)
    vmem = pl.BlockSpec(memory_space=pltpu.VMEM)
    rows, width = blocks[0].shape
    queries = 2 * near.shape[0] * near.shape[2]
    return pl.pallas_call(
        score_kernel,
        out_shape=jax.ShapeDtypeStruct((NX, rows, queries), jnp.float32),
        in_specs=[smem] + [vmem] * 6,
        out_specs=vmem,
        scratch_shapes=[pltpu.VMEM((queries, width), jnp.bfloat16)],
        compiler_params=pltpu.CompilerParams(vmem_limit_bytes=24 * 1024 * 1024),
        name="score",
    )(place, *blocks, near, mate)


def spread(block, members):
    groups = partition(members)
    copies = jnp.broadcast_to(block[None], (len(groups[0]),) + block.shape)
    return lax.all_to_all(copies, AXES, 0, 0, axis_index_groups=groups)


def body(
    query_inputs,
    query_output_grads,
    in_projection,
    out_projection,
    train_grads,
    lengths,
    loss_mask,
    domains,
):
    dp, tensor = lax.axis_index("dp"), lax.axis_index("tensor")
    x, core = dp >> 4, tensor & 1
    layer = x ^ (tensor >> 1)
    place = jnp.stack([x, core]).astype(jnp.int32)

    width = train_grads.shape[1] // LAYERS

    def columns(step):
        return lax.dynamic_slice_in_dim(train_grads, (layer ^ step) * width, width, axis=1)

    blocks = [columns(0)]
    for step in range(1, NX):
        partners = [(flat(a, y, z, c), flat(a ^ step, y, z, c)) for a, y, z, c in places()]
        blocks.append(lax.ppermute(columns(step), AXES, partners))

    parts = project(place, query_inputs, query_output_grads, in_projection, out_projection)
    parts = parts.reshape(2 * LAYERS, -1, 2 * WIDTH)
    parts = lax.all_to_all(parts, "tensor", 0, 0)
    gradient = outer(place, lengths, loss_mask, parts)

    far = spread(gradient, far_members)
    blocks, far = lax.optimization_barrier((blocks, far))
    far = far.transpose(1, 0, 2).reshape(PAIRS, -1, LANES)
    near = spread(far, near_members)
    mates = [(flat(a, y, z, c), flat(a, y, z, 1 - c)) for a, y, z, c in places()]
    mate = lax.ppermute(near, AXES, mates)

    parts = score(place, blocks, near, mate)
    parts = lax.all_to_all(parts, AXES, 0, 0, axis_index_groups=partition(along_x))
    return finish(parts, domains)


def solution(mesh):
    return jax.shard_map(
        body,
        mesh=mesh,
        in_specs=(
            P(None, "dp", None, "tensor"),
            P(None, "dp", None, "tensor"),
            P(None, None, "tensor"),
            P(None, None, "tensor"),
            P(("dp", "tensor"), None),
            P("dp"),
            P("dp", None),
            P(),
        ),
        out_specs=(P(("dp", "tensor"), None), P(("dp", "tensor"), None)),
        check_vma=False,
    )
```

```python
import functools

import jax
import jax.numpy as jnp
from jax import lax
from jax.experimental import pallas as pl
from jax.experimental.pallas import tpu as pltpu
from jax.sharding import PartitionSpec as P

LAYERS = 4
SEQ = 32
WIDTH = 64
DOMAINS = 8
AXES = ("dp", "tensor")
NX, NY, NZ, NC = 4, 8, 8, 2
STEPS = (0, 1, 3, 2)
LANES = 128
PAIRS = WIDTH * WIDTH // LANES


def flat(x, y, z, c):
    return (x * 16 + (y // 4) * 8 + z) * 8 + (y % 4) * 2 + c


def places():
    return [(x, y, z, c) for x in range(NX) for y in range(NY) for z in range(NZ) for c in range(NC)]


def partition(members):
    groups, seen = [], set()
    for place in places():
        group = [flat(*m) for m in members(*place)]
        if group[0] not in seen:
            seen.update(group)
            groups.append(group)
    return groups


def sharing_members(x, y, z, c):
    return [(i, y, z, core) for i in range(NX) for core in range(NC)]


def far_members(x, y, z, c):
    return [
        ((x & 1) | (xh << 1), (h << 2) | ((y & 3) ^ (((x >> 1) ^ xh) << 1)), (z & 1) | (zz << 1), c)
        for xh in range(2)
        for h in range(2)
        for zz in range(4)
    ]


def near_members(x, y, z, c):
    return [
        ((x & 2) | xl, y ^ ((x & 1) ^ xl), (z & 6) | zl, c)
        for xl in range(2)
        for zl in range(2)
    ]


def project_kernel(
    place_ref, in_ref, grad_ref, in_proj_ref, out_proj_ref, out_ref,
    in_buf, grad_buf, in_proj_buf, out_proj_buf, sems,
):
    x = place_ref[0]
    sources = (in_ref, grad_ref, in_proj_ref, out_proj_ref)
    buffers = (in_buf, grad_buf, in_proj_buf, out_proj_buf)
    copies = []
    for j in range(LAYERS):
        copies.append([
            pltpu.make_async_copy(source.at[x ^ j], buffer.at[j], sems.at[j, i])
            for i, (source, buffer) in enumerate(zip(sources, buffers))
        ])
        for copy in copies[j]:
            copy.start()

    def side(rows, proj):
        return lax.dot_general(
            rows.reshape(-1, rows.shape[-1]), proj, (((1,), (1,)), ((), ())), preferred_element_type=jnp.float32
        )

    for j in range(LAYERS):
        for copy in copies[j]:
            copy.wait()
        out_ref[j] = jnp.concatenate([side(in_buf[j], in_proj_buf[j]), side(grad_buf[j], out_proj_buf[j])], axis=1)


def project(place, query_inputs, query_output_grads, in_projection, out_projection):
    _, queries, seq, depth = query_inputs.shape
    hbm = pl.BlockSpec(memory_space=pltpu.HBM)
    return pl.pallas_call(
        project_kernel,
        out_shape=jax.ShapeDtypeStruct((LAYERS, queries * seq, 2 * WIDTH), jnp.float32),
        in_specs=[pl.BlockSpec(memory_space=pltpu.SMEM)] + [hbm] * 4,
        out_specs=pl.BlockSpec(memory_space=pltpu.VMEM),
        scratch_shapes=[
            pltpu.VMEM(query_inputs.shape, query_inputs.dtype),
            pltpu.VMEM(query_inputs.shape, query_inputs.dtype),
            pltpu.VMEM(in_projection.shape, in_projection.dtype),
            pltpu.VMEM(in_projection.shape, in_projection.dtype),
            pltpu.SemaphoreType.DMA((LAYERS, 4)),
        ],
        compiler_params=pltpu.CompilerParams(vmem_limit_bytes=60 * 1024 * 1024),
        name="project",
    )(place, query_inputs, query_output_grads, in_projection, out_projection)


def outer_kernel(place_ref, lengths_ref, mask_ref, parts_ref, out_ref, rows_ref):
    core = place_ref[1]
    total = parts_ref[0]
    for part in range(1, parts_ref.shape[0]):
        total = total + parts_ref[part]
    row = lax.broadcasted_iota(jnp.int32, (SEQ, SEQ), 0)
    col = lax.broadcasted_iota(jnp.int32, (SEQ, SEQ), 1)
    first = lax.broadcasted_iota(jnp.int32, (SEQ, LANES), 1) < WIDTH
    for k in range(2):
        mask = jnp.where(core == 0, mask_ref[k : k + 1, :], mask_ref[2 + k : 3 + k, :])
        kept = (row == col) & (col < lengths_ref[2 * core + k])
        weight = jnp.sum(jnp.where(kept, mask, 0).astype(jnp.float32), axis=1, keepdims=True)
        factors = total[k * SEQ : (k + 1) * SEQ]
        inner = factors[:, :WIDTH]
        inner = jnp.concatenate([inner, inner], axis=1)
        weighted = factors[:, WIDTH:] * weight
        for p in range(PAIRS):
            low = jnp.broadcast_to(weighted[:, 2 * p : 2 * p + 1], (SEQ, LANES))
            high = jnp.broadcast_to(weighted[:, 2 * p + 1 : 2 * p + 2], (SEQ, LANES))
            product = jnp.where(first, low, high) * inner
            rows_ref[2 * p + k : 2 * p + k + 1, :] = jnp.sum(product, axis=0, keepdims=True)
    block = rows_ref[...].astype(jnp.bfloat16)
    for m in range(out_ref.shape[0]):
        out_ref[m] = block


def outer(place, lengths, loss_mask, parts, copies):
    smem = pl.BlockSpec(memory_space=pltpu.SMEM)
    vmem = pl.BlockSpec(memory_space=pltpu.VMEM)
    return pl.pallas_call(
        outer_kernel,
        out_shape=jax.ShapeDtypeStruct((copies, 2 * PAIRS, LANES), jnp.bfloat16),
        in_specs=[smem, smem, vmem, vmem],
        out_specs=vmem,
        scratch_shapes=[pltpu.VMEM((2 * PAIRS, LANES), jnp.float32)],
        compiler_params=pltpu.CompilerParams(vmem_limit_bytes=16 * 1024 * 1024),
        name="outer",
    )(place, lengths, loss_mask, parts)


def finish_kernel(parts_ref, domains_ref, scores_ref, influence_ref):
    def half(core):
        total = parts_ref[core]
        for part in range(core + NC, parts_ref.shape[0], NC):
            total = total + parts_ref[part]
        return total

    total = jnp.concatenate([half(core) for core in range(NC)], axis=1)
    queries = total.shape[1]
    here = lax.broadcasted_iota(jnp.int32, (queries, queries), 0)
    there = lax.broadcasted_iota(jnp.int32, (queries, queries), 1)

    def bit(value, at, to, bits=1):
        return ((value >> at) & ((1 << bits) - 1)) << to

    target = (
        bit(here, 7, 1) + bit(here, 6, 6) + bit(here, 5, 2) + bit(here, 4, 0) + bit(here, 3, 7)
        + bit(here, 2, 5) + bit(here, 0, 3, 2)
    )
    place = (target == there).astype(jnp.float32)
    scores = jnp.dot(total, place, precision=lax.Precision.HIGHEST, preferred_element_type=jnp.float32)
    scores_ref[...] = scores
    lane = lax.broadcasted_iota(jnp.int32, (queries, DOMAINS), 1)
    onehot = (domains_ref[...] == lane).astype(jnp.float32)
    counts = jnp.sum(onehot, axis=0, keepdims=True)
    sums = jnp.dot(scores, onehot, precision=lax.Precision.HIGHEST, preferred_element_type=jnp.float32)
    influence_ref[...] = (sums / counts).T


def finish(parts, domains):
    _, rows, half = parts.shape
    queries = NC * half
    return pl.pallas_call(
        finish_kernel,
        out_shape=(
            jax.ShapeDtypeStruct((rows, queries), jnp.float32),
            jax.ShapeDtypeStruct((DOMAINS, rows), jnp.float32),
        ),
        compiler_params=pltpu.CompilerParams(vmem_limit_bytes=16 * 1024 * 1024),
        name="finish",
    )(parts, domains)


def score_kernel(place_ref, most_ref, last_ref, mate_most_ref, mate_last_ref, near_ref, out_ref, rows_buf, queries_buf):
    x, core = place_ref[0], place_ref[1]
    near, pairs, share, lanes = near_ref.shape
    for n in range(near):
        for p in range(pairs):
            queries_buf[n * share : (n + 1) * share, p * lanes : (p + 1) * lanes] = near_ref[n, p]
    at = 0
    for block_ref in (most_ref, last_ref, mate_most_ref, mate_last_ref):
        rows_buf[at : at + block_ref.shape[0], :] = block_ref[...]
        at += block_ref.shape[0]
    result = lax.dot_general(
        rows_buf[...], queries_buf[...], (((1,), (1,)), ((), ())), preferred_element_type=jnp.float32
    )
    rows = out_ref.shape[1]
    for i in range(NC):
        for n, step in enumerate(STEPS):
            at = (i * NX + n) * rows
            out_ref[pl.ds((x ^ step) * NC + (core ^ i), 1)] = result[at : at + rows][None]


def score(place, most, last, mate_most, mate_last, near):
    smem = pl.BlockSpec(memory_space=pltpu.SMEM)
    vmem = pl.BlockSpec(memory_space=pltpu.VMEM)
    rows, width = last.shape
    queries = near.shape[0] * near.shape[2]
    return pl.pallas_call(
        score_kernel,
        out_shape=jax.ShapeDtypeStruct((NX * NC, rows, queries), jnp.float32),
        in_specs=[smem] + [vmem] * 5,
        out_specs=vmem,
        scratch_shapes=[
            pltpu.VMEM((NX * NC * rows, width), jnp.bfloat16),
            pltpu.VMEM((queries, width), jnp.bfloat16),
        ],
        compiler_params=pltpu.CompilerParams(vmem_limit_bytes=24 * 1024 * 1024),
        name="score",
    )(place, most, last, mate_most, mate_last, near)


def exchange(blocks, members):
    return lax.all_to_all(blocks, AXES, 0, 0, axis_index_groups=partition(members))


def body(
    query_inputs,
    query_output_grads,
    in_projection,
    out_projection,
    train_grads,
    lengths,
    loss_mask,
    domains,
):
    dp, tensor = lax.axis_index("dp"), lax.axis_index("tensor")
    x, core, y_lo = dp >> 4, tensor & 1, tensor >> 1
    place = jnp.stack([x, core]).astype(jnp.int32)
    width = train_grads.shape[1] // LAYERS

    def columns(step):
        return lax.dynamic_slice_in_dim(train_grads, (x ^ y_lo ^ step) * width, width, axis=1)

    def from_x(step):
        return lax.ppermute(columns(step), AXES, [(flat(*p), flat(p[0] ^ step, *p[1:])) for p in places()])

    def from_mate(block):
        return lax.ppermute(block, AXES, [(flat(*p), flat(*p[:3], 1 - p[3])) for p in places()])

    parts = project(place, query_inputs, query_output_grads, in_projection, out_projection)
    parts = parts.reshape(2 * LAYERS, -1, 2 * WIDTH)
    parts = lax.all_to_all(parts, "tensor", 0, 0)
    parts, *most = lax.optimization_barrier((parts, columns(0), from_x(1), from_x(3)))
    most = jnp.concatenate(most, axis=0)

    copies = outer(place, lengths, loss_mask, parts, len(far_members(0, 0, 0, 0)))
    far = exchange(copies, far_members)
    far, last, mate_most = lax.optimization_barrier((far, from_x(2), from_mate(most)))
    far = far.transpose(1, 0, 2).reshape(PAIRS, -1, LANES)
    copies = jnp.broadcast_to(far[None], (4,) + far.shape)
    near = exchange(copies, near_members)
    mate_last = from_mate(last)

    parts = exchange(score(place, most, last, mate_most, mate_last, near), sharing_members)
    scores, influence = finish(parts, domains)
    return scores, influence.T


def solution(mesh):
    return jax.shard_map(
        body,
        mesh=mesh,
        in_specs=(
            P(None, "dp", None, "tensor"),
            P(None, "dp", None, "tensor"),
            P(None, None, "tensor"),
            P(None, None, "tensor"),
            P(("dp", "tensor"), None),
            P("dp"),
            P("dp", None),
            P(),
        ),
        out_specs=(P(("dp", "tensor"), None), P(("dp", "tensor"), None)),
        check_vma=False,
    )
```

```python
import functools

import jax
import jax.numpy as jnp
from jax import lax
from jax.experimental import pallas as pl
from jax.experimental.pallas import tpu as pltpu
from jax.sharding import PartitionSpec as P

LAYERS = 4
SEQ = 32
WIDTH = 64
DOMAINS = 8
AXES = ("dp", "tensor")
NX, NY, NZ, NC = 4, 8, 8, 2
STEPS = (0, 2, 1, 3)
LANES = 128
PAIRS = WIDTH * WIDTH // LANES


def flat(x, y, z, c):
    return (x * 16 + (y // 4) * 8 + z) * 8 + (y % 4) * 2 + c


def places():
    return [(x, y, z, c) for x in range(NX) for y in range(NY) for z in range(NZ) for c in range(NC)]


def partition(members):
    groups, seen = [], set()
    for place in places():
        group = [flat(*m) for m in members(*place)]
        if group[0] not in seen:
            seen.update(group)
            groups.append(group)
    return groups


def sharing_members(x, y, z, c):
    return [(i, y, (z & 6) | zl, core) for i in range(NX) for zl in range(2) for core in range(NC)]


def class_members(x, y, z, c):
    return [
        (i, (h << 2) | ((y & 3) ^ x ^ i), k, c) for i in range(NX) for h in range(2) for k in range(NZ)
    ]


def swapped(block, change):
    return lax.ppermute(block, AXES, [(flat(*change(*p)), flat(*p)) for p in places()])


def swap_x(block, step):
    return swapped(block, lambda x, y, z, c: (x ^ step, y, z, c))


def swap_z(block):
    return swapped(block, lambda x, y, z, c: (x, y, z ^ 1, c))


def swap_core(block):
    return swapped(block, lambda x, y, z, c: (x, y, z, c ^ 1))


def project_kernel(
    place_ref, in_ref, grad_ref, in_proj_ref, out_proj_ref, out_ref,
    in_buf, grad_buf, in_proj_buf, out_proj_buf, sems,
):
    x = place_ref[0]
    sources = (in_ref, grad_ref, in_proj_ref, out_proj_ref)
    buffers = (in_buf, grad_buf, in_proj_buf, out_proj_buf)
    copies = []
    for j in range(LAYERS):
        copies.append([
            pltpu.make_async_copy(source.at[x ^ j], buffer.at[j], sems.at[j, i])
            for i, (source, buffer) in enumerate(zip(sources, buffers))
        ])
        for copy in copies[j]:
            copy.start()

    def side(rows, proj):
        return lax.dot_general(
            rows.reshape(-1, rows.shape[-1]), proj, (((1,), (1,)), ((), ())), preferred_element_type=jnp.float32
        )

    for j in range(LAYERS):
        for copy in copies[j]:
            copy.wait()
        out_ref[j] = jnp.concatenate([side(in_buf[j], in_proj_buf[j]), side(grad_buf[j], out_proj_buf[j])], axis=1)


def project(place, query_inputs, query_output_grads, in_projection, out_projection):
    _, queries, seq, depth = query_inputs.shape
    hbm = pl.BlockSpec(memory_space=pltpu.HBM)
    return pl.pallas_call(
        project_kernel,
        out_shape=jax.ShapeDtypeStruct((LAYERS, queries * seq, 2 * WIDTH), jnp.float32),
        in_specs=[pl.BlockSpec(memory_space=pltpu.SMEM)] + [hbm] * 4,
        out_specs=pl.BlockSpec(memory_space=pltpu.VMEM),
        scratch_shapes=[
            pltpu.VMEM(query_inputs.shape, query_inputs.dtype),
            pltpu.VMEM(query_inputs.shape, query_inputs.dtype),
            pltpu.VMEM(in_projection.shape, in_projection.dtype),
            pltpu.VMEM(in_projection.shape, in_projection.dtype),
            pltpu.SemaphoreType.DMA((LAYERS, 4)),
        ],
        compiler_params=pltpu.CompilerParams(vmem_limit_bytes=60 * 1024 * 1024),
        name="project",
    )(place, query_inputs, query_output_grads, in_projection, out_projection)


def outer_kernel(place_ref, lengths_ref, mask_ref, parts_ref, out_ref, rows_ref):
    core = place_ref[1]
    total = parts_ref[0]
    for part in range(1, parts_ref.shape[0]):
        total = total + parts_ref[part]
    row = lax.broadcasted_iota(jnp.int32, (SEQ, SEQ), 0)
    col = lax.broadcasted_iota(jnp.int32, (SEQ, SEQ), 1)
    first = lax.broadcasted_iota(jnp.int32, (SEQ, LANES), 1) < WIDTH
    for k in range(2):
        mask = jnp.where(core == 0, mask_ref[k : k + 1, :], mask_ref[2 + k : 3 + k, :])
        kept = (row == col) & (col < lengths_ref[2 * core + k])
        weight = jnp.sum(jnp.where(kept, mask, 0).astype(jnp.float32), axis=1, keepdims=True)
        factors = total[k * SEQ : (k + 1) * SEQ]
        inner = factors[:, :WIDTH]
        inner = jnp.concatenate([inner, inner], axis=1)
        weighted = factors[:, WIDTH:] * weight
        for p in range(PAIRS):
            low = jnp.broadcast_to(weighted[:, 2 * p : 2 * p + 1], (SEQ, LANES))
            high = jnp.broadcast_to(weighted[:, 2 * p + 1 : 2 * p + 2], (SEQ, LANES))
            product = jnp.where(first, low, high) * inner
            rows_ref[2 * p + k : 2 * p + k + 1, :] = jnp.sum(product, axis=0, keepdims=True)
    block = rows_ref[...].astype(jnp.bfloat16)
    half = out_ref.shape[1]
    for m in range(out_ref.shape[0]):
        out_ref[m] = block[(m & 1) * half : (m & 1) * half + half]


def outer(place, lengths, loss_mask, parts, members):
    smem = pl.BlockSpec(memory_space=pltpu.SMEM)
    vmem = pl.BlockSpec(memory_space=pltpu.VMEM)
    return pl.pallas_call(
        outer_kernel,
        out_shape=jax.ShapeDtypeStruct((members, PAIRS, LANES), jnp.bfloat16),
        in_specs=[smem, smem, vmem, vmem],
        out_specs=vmem,
        scratch_shapes=[pltpu.VMEM((2 * PAIRS, LANES), jnp.float32)],
        compiler_params=pltpu.CompilerParams(vmem_limit_bytes=16 * 1024 * 1024),
        cost_estimate=pl.CostEstimate(flops=0, bytes_accessed=60 * 1024 * 1024, transcendentals=0),
        name="outer",
    )(place, lengths, loss_mask, parts)


def finish_kernel(parts_ref, domains_ref, scores_ref, influence_ref):
    def half(core):
        total = parts_ref[core]
        for part in range(core + NC, parts_ref.shape[0], NC):
            total = total + parts_ref[part]
        return total

    total = jnp.concatenate([half(core) for core in range(NC)], axis=1)
    queries = total.shape[1]
    here = lax.broadcasted_iota(jnp.int32, (queries, queries), 0)
    there = lax.broadcasted_iota(jnp.int32, (queries, queries), 1)
    target = ((here & 63) << 2) + ((here >> 7) << 1) + ((here >> 6) & 1)
    place = (target == there).astype(jnp.float32)
    scores = jnp.dot(total, place, precision=lax.Precision.HIGHEST, preferred_element_type=jnp.float32)
    scores_ref[...] = scores
    lane = lax.broadcasted_iota(jnp.int32, (queries, DOMAINS), 1)
    onehot = (domains_ref[...] == lane).astype(jnp.float32)
    counts = jnp.sum(onehot, axis=0, keepdims=True)
    sums = jnp.dot(scores, onehot, precision=lax.Precision.HIGHEST, preferred_element_type=jnp.float32)
    influence_ref[...] = (sums / counts).T


def finish(parts, domains):
    _, rows, half = parts.shape
    queries = NC * half
    return pl.pallas_call(
        finish_kernel,
        out_shape=(
            jax.ShapeDtypeStruct((rows, queries), jnp.float32),
            jax.ShapeDtypeStruct((DOMAINS, rows), jnp.float32),
        ),
        compiler_params=pltpu.CompilerParams(vmem_limit_bytes=16 * 1024 * 1024),
        name="finish",
    )(parts, domains)


def score_kernel(place_ref, *refs):
    *rows_refs, blocks_ref, out_ref, rows_buf, queries_buf = refs
    x, core, z_low = place_ref[0], place_ref[1], place_ref[2]
    lines, sources, lanes = blocks_ref.shape
    for line in range(lines):
        pair, query = line // 2, line % 2
        queries_buf[query * sources : (query + 1) * sources, pair * lanes : (pair + 1) * lanes] = blocks_ref[line]
    at = 0
    for ref in rows_refs:
        rows_buf[at : at + ref.shape[0], :] = ref[...]
        at += ref.shape[0]
    result = lax.dot_general(
        rows_buf[...], queries_buf[...], (((1,), (1,)), ((), ())), preferred_element_type=jnp.float32
    )
    rows = out_ref.shape[1]
    at = 0
    for other_core in range(NC):
        for step in STEPS:
            for other_z in range(2):
                member = ((x ^ step) * 2 + (z_low ^ other_z)) * NC + (core ^ other_core)
                out_ref[pl.ds(member, 1)] = result[at : at + rows][None]
                at += rows


def score(place, rows, blocks):
    smem = pl.BlockSpec(memory_space=pltpu.SMEM)
    vmem = pl.BlockSpec(memory_space=pltpu.VMEM)
    count = sum(block.shape[0] for block in rows)
    width = rows[0].shape[1]
    members = 2 * NX * NC
    queries = 2 * blocks.shape[1]
    return pl.pallas_call(
        score_kernel,
        out_shape=jax.ShapeDtypeStruct((members, count // members, queries), jnp.float32),
        in_specs=[smem] + [vmem] * (len(rows) + 1),
        out_specs=vmem,
        scratch_shapes=[
            pltpu.VMEM((count, width), jnp.bfloat16),
            pltpu.VMEM((queries, width), jnp.bfloat16),
        ],
        compiler_params=pltpu.CompilerParams(vmem_limit_bytes=24 * 1024 * 1024),
        name="score",
    )(place, *rows, blocks)


def after(block, *others):
    return lax.optimization_barrier((block,) + others)[0]


def exchange(blocks, members):
    return lax.all_to_all(blocks, AXES, 0, 0, axis_index_groups=partition(members))


def body(
    query_inputs,
    query_output_grads,
    in_projection,
    out_projection,
    train_grads,
    lengths,
    loss_mask,
    domains,
):
    dp, tensor = lax.axis_index("dp"), lax.axis_index("tensor")
    x, z_low, core, y_lo = dp >> 4, dp & 1, tensor & 1, tensor >> 1
    place = jnp.stack([x, core, z_low]).astype(jnp.int32)
    count, ktot = train_grads.shape
    width = ktot // LAYERS // 2

    def half(which):
        return jnp.concatenate(
            [lax.dynamic_slice_in_dim(train_grads, (2 * i + which) * width, width, axis=1) for i in range(LAYERS)], axis=1
        )

    kept, other = half(z_low), swap_z(half(1 - z_low))

    def columns(step):
        at = (x ^ y_lo ^ step) * width
        return jnp.concatenate(
            [lax.dynamic_slice_in_dim(block, at, width, axis=1) for block in (kept, other)], axis=0
        )

    layer = lax.dynamic_slice_in_dim(train_grads, (x ^ y_lo ^ 2) * 2 * width, 2 * width, axis=1)
    layer = after(swap_x(layer, 2), other)
    parts = project(place, query_inputs, query_output_grads, in_projection, out_projection)
    parts = parts.reshape(2 * LAYERS, -1, 2 * WIDTH)

    parts = lax.all_to_all(parts, "tensor", 0, 0)

    across = [
        lax.dynamic_slice_in_dim(layer, z_low * width, width, axis=1),
        swap_z(lax.dynamic_slice_in_dim(layer, (1 - z_low) * width, width, axis=1)),
    ]

    rows = [
        jnp.concatenate([columns(0)] + across, axis=0),
        jnp.concatenate([swap_x(columns(step), step) for step in STEPS[2:]], axis=0),
    ]
    blocks = outer(place, lengths, loss_mask, parts, len(class_members(0, 0, 0, 0)))

    blocks = exchange(blocks, class_members)
    blocks = blocks.transpose(1, 0, 2)
    rows += [swap_core(block) for block in rows]

    parts = exchange(score(place, rows, blocks), sharing_members)
    scores, influence = finish(parts, domains)
    return scores, influence.T


def solution(mesh):
    return jax.shard_map(
        body,
        mesh=mesh,
        in_specs=(
            P(None, "dp", None, "tensor"),
            P(None, "dp", None, "tensor"),
            P(None, None, "tensor"),
            P(None, None, "tensor"),
            P(("dp", "tensor"), None),
            P("dp"),
            P("dp", None),
            P(),
        ),
        out_specs=(P(("dp", "tensor"), None), P(("dp", "tensor"), None)),
        check_vma=False,
    )
```

```python
import functools

import jax
import jax.numpy as jnp
from jax import lax
from jax.experimental import pallas as pl
from jax.experimental.pallas import tpu as pltpu
from jax.sharding import PartitionSpec as P

LAYERS = 4
SEQ = 32
WIDTH = 64
DOMAINS = 8
AXES = ("dp", "tensor")
NX, NY, NZ, NC = 4, 8, 8, 2
STEPS = (0, 2, 1, 3)
LANES = 128
PAIRS = WIDTH * WIDTH // LANES


def flat(x, y, z, c):
    return (x * 16 + (y // 4) * 8 + z) * 8 + (y % 4) * 2 + c


def places():
    return [(x, y, z, c) for x in range(NX) for y in range(NY) for z in range(NZ) for c in range(NC)]


def partition(members):
    groups, seen = [], set()
    for place in places():
        group = [flat(*m) for m in members(*place)]
        if group[0] not in seen:
            seen.update(group)
            groups.append(group)
    return groups


def sharing_members(x, y, z, c):
    return [(i, y, (z & 6) | zl, core) for i in range(NX) for zl in range(2) for core in range(NC)]


def class_members(x, y, z, c):
    return [
        (i, (h << 2) | ((y & 3) ^ x ^ i), k, c) for i in range(NX) for h in range(2) for k in range(NZ)
    ]


def swapped(block, change):
    return lax.ppermute(block, AXES, [(flat(*change(*p)), flat(*p)) for p in places()])


def swap_x(block, step):
    return swapped(block, lambda x, y, z, c: (x ^ step, y, z, c))


def swap_z(block):
    return swapped(block, lambda x, y, z, c: (x, y, z ^ 1, c))


def swap_core(block):
    return swapped(block, lambda x, y, z, c: (x, y, z, c ^ 1))


def here():
    dp, tensor = lax.axis_index("dp"), lax.axis_index("tensor")
    return dp >> 4, tensor >> 1, dp & 1, tensor & 1


def project_kernel(
    in_ref, grad_ref, in_proj_ref, out_proj_ref, out_ref, in_buf, grad_buf, in_proj_buf, out_proj_buf, sems
):
    x, _, _, _ = here()
    sources = (in_ref, grad_ref, in_proj_ref, out_proj_ref)
    buffers = (in_buf, grad_buf, in_proj_buf, out_proj_buf)
    copies = []
    for layer in range(LAYERS):
        copies.append([
            pltpu.make_async_copy(source.at[layer], buffer.at[layer], sems.at[layer, i])
            for i, (source, buffer) in enumerate(zip(sources, buffers))
        ])
        for copy in copies[layer]:
            copy.start()

    def side(rows, proj):
        return lax.dot_general(
            rows.reshape(-1, rows.shape[-1]), proj, (((1,), (1,)), ((), ())), preferred_element_type=jnp.float32
        )

    for layer in range(LAYERS):
        for copy in copies[layer]:
            copy.wait()
        both = [side(in_buf[layer], in_proj_buf[layer]), side(grad_buf[layer], out_proj_buf[layer])]
        out_ref[pl.ds(x ^ layer, 1)] = jnp.concatenate(both, axis=1)[None]


def project(query_inputs, query_output_grads, in_projection, out_projection):
    _, queries, seq, depth = query_inputs.shape
    hbm = pl.BlockSpec(memory_space=pltpu.HBM)
    return pl.pallas_call(
        project_kernel,
        out_shape=jax.ShapeDtypeStruct((LAYERS, queries * seq, 2 * WIDTH), jnp.float32),
        in_specs=[hbm] * 4,
        out_specs=pl.BlockSpec(memory_space=pltpu.VMEM),
        scratch_shapes=[
            pltpu.VMEM(query_inputs.shape, query_inputs.dtype),
            pltpu.VMEM(query_inputs.shape, query_inputs.dtype),
            pltpu.VMEM(in_projection.shape, in_projection.dtype),
            pltpu.VMEM(in_projection.shape, in_projection.dtype),
            pltpu.SemaphoreType.DMA((LAYERS, 4)),
        ],
        compiler_params=pltpu.CompilerParams(vmem_limit_bytes=60 * 1024 * 1024),
        name="project",
    )(query_inputs, query_output_grads, in_projection, out_projection)


def outer_kernel(lengths_ref, mask_ref, parts_ref, out_ref, rows_ref):
    _, _, _, core = here()
    total = parts_ref[0]
    for part in range(1, parts_ref.shape[0]):
        total = total + parts_ref[part]
    row = lax.broadcasted_iota(jnp.int32, (SEQ, SEQ), 0)
    col = lax.broadcasted_iota(jnp.int32, (SEQ, SEQ), 1)
    first = lax.broadcasted_iota(jnp.int32, (SEQ, LANES), 1) < WIDTH
    for k in range(2):
        mask = jnp.where(core == 0, mask_ref[k : k + 1, :], mask_ref[2 + k : 3 + k, :])
        kept = (row == col) & (col < lengths_ref[2 * core + k])
        weight = jnp.sum(jnp.where(kept, mask, 0).astype(jnp.float32), axis=1, keepdims=True)
        factors = total[k * SEQ : (k + 1) * SEQ]
        inner = factors[:, :WIDTH]
        inner = jnp.concatenate([inner, inner], axis=1)
        weighted = factors[:, WIDTH:] * weight
        for p in range(PAIRS):
            low = jnp.broadcast_to(weighted[:, 2 * p : 2 * p + 1], (SEQ, LANES))
            high = jnp.broadcast_to(weighted[:, 2 * p + 1 : 2 * p + 2], (SEQ, LANES))
            product = jnp.where(first, low, high) * inner
            rows_ref[2 * p + k : 2 * p + k + 1, :] = jnp.sum(product, axis=0, keepdims=True)
    block = rows_ref[...].astype(jnp.bfloat16)
    half = out_ref.shape[1]
    for m in range(out_ref.shape[0]):
        out_ref[m] = block[(m & 1) * half : (m & 1) * half + half]


def outer(lengths, loss_mask, parts, members):
    smem = pl.BlockSpec(memory_space=pltpu.SMEM)
    vmem = pl.BlockSpec(memory_space=pltpu.VMEM)
    return pl.pallas_call(
        outer_kernel,
        out_shape=jax.ShapeDtypeStruct((members, PAIRS, LANES), jnp.bfloat16),
        in_specs=[smem, vmem, vmem],
        out_specs=vmem,
        scratch_shapes=[pltpu.VMEM((2 * PAIRS, LANES), jnp.float32)],
        compiler_params=pltpu.CompilerParams(vmem_limit_bytes=16 * 1024 * 1024),
        cost_estimate=pl.CostEstimate(flops=0, bytes_accessed=60 * 1024 * 1024, transcendentals=0),
        name="outer",
    )(lengths, loss_mask, parts)


def finish_kernel(parts_ref, domains_ref, scores_ref, influence_ref):
    def half(core):
        total = parts_ref[core]
        for part in range(core + NC, parts_ref.shape[0], NC):
            total = total + parts_ref[part]
        return total

    total = jnp.concatenate([half(core) for core in range(NC)], axis=1)
    queries = total.shape[1]
    column = lax.broadcasted_iota(jnp.int32, (queries, queries), 0)
    there = lax.broadcasted_iota(jnp.int32, (queries, queries), 1)
    target = ((column & 63) << 2) + ((column >> 7) << 1) + ((column >> 6) & 1)
    place = (target == there).astype(jnp.float32)
    scores = jnp.dot(total, place, precision=lax.Precision.HIGHEST, preferred_element_type=jnp.float32)
    scores_ref[...] = scores
    lane = lax.broadcasted_iota(jnp.int32, (queries, DOMAINS), 1)
    onehot = (domains_ref[...] == lane).astype(jnp.float32)
    counts = jnp.sum(onehot, axis=0, keepdims=True)
    sums = jnp.dot(scores, onehot, precision=lax.Precision.HIGHEST, preferred_element_type=jnp.float32)
    influence_ref[...] = (sums / counts).T


def finish(parts, domains):
    _, rows, half = parts.shape
    queries = NC * half
    return pl.pallas_call(
        finish_kernel,
        out_shape=(
            jax.ShapeDtypeStruct((rows, queries), jnp.float32),
            jax.ShapeDtypeStruct((DOMAINS, rows), jnp.float32),
        ),
        compiler_params=pltpu.CompilerParams(vmem_limit_bytes=16 * 1024 * 1024),
        name="finish",
    )(parts, domains)


def score_kernel(*refs):
    *rows_refs, blocks_ref, out_ref, rows_buf, queries_buf = refs
    x, _, z_low, core = here()
    lines, sources, lanes = blocks_ref.shape
    for line in range(lines):
        pair, query = line // 2, line % 2
        queries_buf[query * sources : (query + 1) * sources, pair * lanes : (pair + 1) * lanes] = blocks_ref[line]
    at = 0
    for ref in rows_refs:
        rows_buf[at : at + ref.shape[0], :] = ref[...]
        at += ref.shape[0]
    result = lax.dot_general(
        rows_buf[...], queries_buf[...], (((1,), (1,)), ((), ())), preferred_element_type=jnp.float32
    )
    rows = out_ref.shape[1]
    at = 0
    for other_core in range(NC):
        for step in STEPS:
            for other_z in range(2):
                member = ((x ^ step) * 2 + (z_low ^ other_z)) * NC + (core ^ other_core)
                out_ref[pl.ds(member, 1)] = result[at : at + rows][None]
                at += rows


def score(rows, blocks):
    vmem = pl.BlockSpec(memory_space=pltpu.VMEM)
    count = sum(block.shape[0] for block in rows)
    width = rows[0].shape[1]
    members = 2 * NX * NC
    queries = 2 * blocks.shape[1]
    return pl.pallas_call(
        score_kernel,
        out_shape=jax.ShapeDtypeStruct((members, count // members, queries), jnp.float32),
        in_specs=[vmem] * (len(rows) + 1),
        out_specs=vmem,
        scratch_shapes=[
            pltpu.VMEM((count, width), jnp.bfloat16),
            pltpu.VMEM((queries, width), jnp.bfloat16),
        ],
        compiler_params=pltpu.CompilerParams(vmem_limit_bytes=24 * 1024 * 1024),
        name="score",
    )(*rows, blocks)


def after(block, *others):
    return lax.optimization_barrier((block,) + others)[0]


def exchange(blocks, members):
    return lax.all_to_all(blocks, AXES, 0, 0, axis_index_groups=partition(members))


def body(
    query_inputs,
    query_output_grads,
    in_projection,
    out_projection,
    train_grads,
    lengths,
    loss_mask,
    domains,
):
    x, y_lo, z_low, _ = here()
    count, ktot = train_grads.shape
    width = ktot // LAYERS // 2

    def half(which):
        return jnp.concatenate(
            [lax.dynamic_slice_in_dim(train_grads, (2 * i + which) * width, width, axis=1) for i in range(LAYERS)], axis=1
        )

    kept, other = half(z_low), swap_z(half(1 - z_low))

    def columns(step):
        at = (x ^ y_lo ^ step) * width
        return jnp.concatenate(
            [lax.dynamic_slice_in_dim(block, at, width, axis=1) for block in (kept, other)], axis=0
        )

    layer = lax.dynamic_slice_in_dim(train_grads, (x ^ y_lo ^ 2) * 2 * width, 2 * width, axis=1)
    layer = after(swap_x(layer, 2), other)
    parts = project(query_inputs, query_output_grads, in_projection, out_projection)
    parts = parts.reshape(2 * LAYERS, -1, 2 * WIDTH)
    parts = lax.all_to_all(parts, "tensor", 0, 0)

    across = [
        lax.dynamic_slice_in_dim(layer, z_low * width, width, axis=1),
        swap_z(lax.dynamic_slice_in_dim(layer, (1 - z_low) * width, width, axis=1)),
    ]

    rows = [
        jnp.concatenate([columns(0)] + across, axis=0),
        jnp.concatenate([swap_x(columns(step), step) for step in STEPS[2:]], axis=0),
    ]
    blocks = outer(lengths, loss_mask, parts, len(class_members(0, 0, 0, 0)))
    blocks = exchange(blocks, class_members)
    blocks = blocks.transpose(1, 0, 2)
    rows += [swap_core(block) for block in rows]

    parts = exchange(score(rows, blocks), sharing_members)
    scores, influence = finish(parts, domains)
    return scores, influence.T


def solution(mesh):
    return jax.shard_map(
        body,
        mesh=mesh,
        in_specs=(
            P(None, "dp", None, "tensor"),
            P(None, "dp", None, "tensor"),
            P(None, None, "tensor"),
            P(None, None, "tensor"),
            P(("dp", "tensor"), None),
            P("dp"),
            P("dp", None),
            P(),
        ),
        out_specs=(P(("dp", "tensor"), None), P(("dp", "tensor"), None)),
        check_vma=False,
    )
```

```python
import functools

import jax
import jax.numpy as jnp
from jax import lax
from jax.experimental import pallas as pl
from jax.experimental.pallas import tpu as pltpu
from jax.sharding import PartitionSpec as P

LAYERS = 4
SEQ = 32
WIDTH = 64
DOMAINS = 8
AXES = ("dp", "tensor")
NX, NY, NZ, NC = 4, 8, 8, 2
ORDER = ((0, 0), (0, 1), (2, 0), (1, 0), (1, 1), (3, 0), (3, 1), (2, 1))
LANES = 128
PAIRS = WIDTH * WIDTH // LANES


def flat(x, y, z, c):
    return (x * 16 + (y // 4) * 8 + z) * 8 + (y % 4) * 2 + c


def places():
    return [(x, y, z, c) for x in range(NX) for y in range(NY) for z in range(NZ) for c in range(NC)]


def partition(members):
    groups, seen = [], set()
    for place in places():
        group = [flat(*m) for m in members(*place)]
        if group[0] not in seen:
            seen.update(group)
            groups.append(group)
    return groups


def sharing_members(x, y, z, c):
    return [(i, y, (z & 6) | zl, core) for i in range(NX) for zl in range(2) for core in range(NC)]


def class_members(x, y, z, c):
    return [
        (i, (h << 2) | ((y & 3) ^ x ^ i), k, c) for i in range(NX) for h in range(2) for k in range(NZ)
    ]


def swapped(block, change):
    return lax.ppermute(block, AXES, [(flat(*change(*p)), flat(*p)) for p in places()])


def swap_x(block, step):
    return swapped(block, lambda x, y, z, c: (x ^ step, y, z, c))


def swap_z(block):
    return swapped(block, lambda x, y, z, c: (x, y, z ^ 1, c))


def swap_core(block):
    return swapped(block, lambda x, y, z, c: (x, y, z, c ^ 1))


def here():
    dp, tensor = lax.axis_index("dp"), lax.axis_index("tensor")
    return dp >> 4, tensor >> 1, dp & 1, tensor & 1


def project_kernel(
    in_ref, grad_ref, in_proj_ref, out_proj_ref, out_ref, in_buf, grad_buf, in_proj_buf, out_proj_buf, sems
):
    x, _, _, _ = here()
    sources = (in_ref, grad_ref, in_proj_ref, out_proj_ref)
    buffers = (in_buf, grad_buf, in_proj_buf, out_proj_buf)
    copies = []
    for layer in range(LAYERS):
        copies.append([
            pltpu.make_async_copy(source.at[layer], buffer.at[layer], sems.at[layer, i])
            for i, (source, buffer) in enumerate(zip(sources, buffers))
        ])
        for copy in copies[layer]:
            copy.start()

    def side(rows, proj):
        return lax.dot_general(
            rows.reshape(-1, rows.shape[-1]), proj, (((1,), (1,)), ((), ())), preferred_element_type=jnp.float32
        )

    for layer in range(LAYERS):
        for copy in copies[layer]:
            copy.wait()
        both = [side(in_buf[layer], in_proj_buf[layer]), side(grad_buf[layer], out_proj_buf[layer])]
        out_ref[pl.ds(x ^ layer, 1)] = jnp.concatenate(both, axis=1)[None]


def project(query_inputs, query_output_grads, in_projection, out_projection):
    _, queries, seq, depth = query_inputs.shape
    hbm = pl.BlockSpec(memory_space=pltpu.HBM)
    return pl.pallas_call(
        project_kernel,
        out_shape=jax.ShapeDtypeStruct((LAYERS, queries * seq, 2 * WIDTH), jnp.float32),
        in_specs=[hbm] * 4,
        out_specs=pl.BlockSpec(memory_space=pltpu.VMEM),
        scratch_shapes=[
            pltpu.VMEM(query_inputs.shape, query_inputs.dtype),
            pltpu.VMEM(query_inputs.shape, query_inputs.dtype),
            pltpu.VMEM(in_projection.shape, in_projection.dtype),
            pltpu.VMEM(in_projection.shape, in_projection.dtype),
            pltpu.SemaphoreType.DMA((LAYERS, 4)),
        ],
        compiler_params=pltpu.CompilerParams(vmem_limit_bytes=60 * 1024 * 1024),
        name="project",
    )(query_inputs, query_output_grads, in_projection, out_projection)


def outer_kernel(lengths_ref, mask_ref, parts_ref, out_ref, rows_ref, blocks_buf, sems):
    _, _, _, core = here()
    total = parts_ref[0]
    for part in range(1, parts_ref.shape[0]):
        total = total + parts_ref[part]
    row = lax.broadcasted_iota(jnp.int32, (SEQ, SEQ), 0)
    col = lax.broadcasted_iota(jnp.int32, (SEQ, SEQ), 1)
    first = lax.broadcasted_iota(jnp.int32, (SEQ, LANES), 1) < WIDTH
    inner, weighted = [], []
    for k in range(2):
        mask = jnp.where(core == 0, mask_ref[k : k + 1, :], mask_ref[2 + k : 3 + k, :])
        kept = (row == col) & (col < lengths_ref[2 * core + k])
        weight = jnp.sum(jnp.where(kept, mask, 0).astype(jnp.float32), axis=1, keepdims=True)
        factors = total[k * SEQ : (k + 1) * SEQ]
        inner.append(jnp.concatenate([factors[:, :WIDTH]] * 2, axis=1))
        weighted.append(factors[:, WIDTH:] * weight)
    members, half, _ = blocks_buf.shape[1:]
    copies = []
    for part in range(2):
        for p in range(part * half // 2, (part + 1) * half // 2):
            for k in range(2):
                low = jnp.broadcast_to(weighted[k][:, 2 * p : 2 * p + 1], (SEQ, LANES))
                high = jnp.broadcast_to(weighted[k][:, 2 * p + 1 : 2 * p + 2], (SEQ, LANES))
                product = jnp.where(first, low, high) * inner[k]
                rows_ref[2 * p + k : 2 * p + k + 1, :] = jnp.sum(product, axis=0, keepdims=True)
        block = rows_ref[part * half : (part + 1) * half, :].astype(jnp.bfloat16)
        for m in range(members):
            blocks_buf[part, m] = block
        copies.append(pltpu.make_async_copy(blocks_buf.at[part], out_ref.at[:, part], sems.at[part]))
        copies[part].start()
    for copy in copies:
        copy.wait()


def outer(lengths, loss_mask, parts, members):
    vmem = pl.BlockSpec(memory_space=pltpu.VMEM)
    blocks = pl.pallas_call(
        outer_kernel,
        out_shape=jax.ShapeDtypeStruct((members // 2, 2, PAIRS, LANES), jnp.bfloat16),
        in_specs=[pl.BlockSpec(memory_space=pltpu.SMEM), vmem, vmem],
        out_specs=pl.BlockSpec(memory_space=pltpu.HBM),
        scratch_shapes=[
            pltpu.VMEM((2 * PAIRS, LANES), jnp.float32),
            pltpu.VMEM((2, members // 2, PAIRS, LANES), jnp.bfloat16),
            pltpu.SemaphoreType.DMA((2,)),
        ],
        compiler_params=pltpu.CompilerParams(vmem_limit_bytes=16 * 1024 * 1024),
        cost_estimate=pl.CostEstimate(flops=0, bytes_accessed=60 * 1024 * 1024, transcendentals=0),
        name="outer",
    )(lengths, loss_mask, parts)
    return blocks.reshape(members, PAIRS, LANES)


def finish_kernel(parts_ref, domains_ref, scores_ref, influence_ref):
    def half(core):
        total = parts_ref[core]
        for part in range(core + NC, parts_ref.shape[0], NC):
            total = total + parts_ref[part]
        return total

    total = jnp.concatenate([half(core) for core in range(NC)], axis=1)
    queries = total.shape[1]
    column = lax.broadcasted_iota(jnp.int32, (queries, queries), 0)
    there = lax.broadcasted_iota(jnp.int32, (queries, queries), 1)
    target = ((column & 63) << 2) + ((column >> 7) << 1) + ((column >> 6) & 1)
    place = (target == there).astype(jnp.float32)
    scores = jnp.dot(total, place, precision=lax.Precision.HIGHEST, preferred_element_type=jnp.float32)
    scores_ref[...] = scores
    lane = lax.broadcasted_iota(jnp.int32, (queries, DOMAINS), 1)
    onehot = (domains_ref[...] == lane).astype(jnp.float32)
    counts = jnp.sum(onehot, axis=0, keepdims=True)
    sums = jnp.dot(scores, onehot, precision=lax.Precision.HIGHEST, preferred_element_type=jnp.float32)
    influence_ref[...] = (sums / counts).T


def finish(parts, domains):
    _, rows, half = parts.shape
    queries = NC * half
    return pl.pallas_call(
        finish_kernel,
        out_shape=(
            jax.ShapeDtypeStruct((rows, queries), jnp.float32),
            jax.ShapeDtypeStruct((DOMAINS, rows), jnp.float32),
        ),
        compiler_params=pltpu.CompilerParams(vmem_limit_bytes=16 * 1024 * 1024),
        name="finish",
    )(parts, domains)


def score_kernel(*refs):
    *rows_refs, blocks_ref, out_ref, rows_buf, queries_buf = refs
    x, _, z_low, core = here()
    lines, sources, lanes = blocks_ref.shape
    for line in range(lines):
        pair, query = line // 2, line % 2
        queries_buf[query * sources : (query + 1) * sources, pair * lanes : (pair + 1) * lanes] = blocks_ref[line]
    at = 0
    for ref in rows_refs:
        rows_buf[at : at + ref.shape[0], :] = ref[...]
        at += ref.shape[0]
    result = lax.dot_general(
        rows_buf[...], queries_buf[...], (((1,), (1,)), ((), ())), preferred_element_type=jnp.float32
    )
    rows = out_ref.shape[1]
    at = 0
    for other_core in range(NC):
        for step, other_z in ORDER:
            member = ((x ^ step) * 2 + (z_low ^ other_z)) * NC + (core ^ other_core)
            out_ref[pl.ds(member, 1)] = result[at : at + rows][None]
            at += rows


def score(rows, blocks):
    vmem = pl.BlockSpec(memory_space=pltpu.VMEM)
    count = sum(block.shape[0] for block in rows)
    width = rows[0].shape[1]
    members = 2 * NX * NC
    queries = 2 * blocks.shape[1]
    return pl.pallas_call(
        score_kernel,
        out_shape=jax.ShapeDtypeStruct((members, count // members, queries), jnp.float32),
        in_specs=[vmem] * (len(rows) + 1),
        out_specs=vmem,
        scratch_shapes=[
            pltpu.VMEM((count, width), jnp.bfloat16),
            pltpu.VMEM((queries, width), jnp.bfloat16),
        ],
        compiler_params=pltpu.CompilerParams(vmem_limit_bytes=24 * 1024 * 1024),
        name="score",
    )(*rows, blocks)


def after(block, *others):
    return lax.optimization_barrier((block,) + others)[0]


def exchange(blocks, members):
    return lax.all_to_all(blocks, AXES, 0, 0, axis_index_groups=partition(members))


def body(
    query_inputs,
    query_output_grads,
    in_projection,
    out_projection,
    train_grads,
    lengths,
    loss_mask,
    domains,
):
    x, y_lo, z_low, _ = here()
    count, ktot = train_grads.shape
    width = ktot // LAYERS // 2

    def half(which):
        return jnp.concatenate(
            [lax.dynamic_slice_in_dim(train_grads, (2 * i + which) * width, width, axis=1) for i in range(LAYERS)], axis=1
        )

    kept, other = half(z_low), swap_z(half(1 - z_low))

    def columns(step):
        at = (x ^ y_lo ^ step) * width
        return jnp.concatenate(
            [lax.dynamic_slice_in_dim(block, at, width, axis=1) for block in (kept, other)], axis=0
        )

    layer = lax.dynamic_slice_in_dim(train_grads, (x ^ y_lo ^ 2) * 2 * width, 2 * width, axis=1)
    layer = after(swap_x(layer, 2), other)
    parts = project(query_inputs, query_output_grads, in_projection, out_projection)
    parts = parts.reshape(2 * LAYERS, -1, 2 * WIDTH)
    parts = lax.all_to_all(parts, "tensor", 0, 0)

    across = [
        lax.dynamic_slice_in_dim(layer, z_low * width, width, axis=1),
        swap_z(lax.dynamic_slice_in_dim(layer, (1 - z_low) * width, width, axis=1)),
    ]

    ring = [swap_x(columns(step), step) for step in (1, 3)]
    rows = [
        jnp.concatenate([columns(0), across[0], ring[0]], axis=0),
        jnp.concatenate([ring[1], across[1]], axis=0),
    ]
    blocks = outer(lengths, loss_mask, parts, len(class_members(0, 0, 0, 0)))
    blocks = exchange(blocks, class_members)
    blocks = blocks.transpose(1, 0, 2)
    rows += [swap_core(block) for block in rows]

    parts = exchange(score(rows, blocks), sharing_members)
    scores, influence = finish(parts, domains)
    return scores, influence.T


def solution(mesh):
    return jax.shard_map(
        body,
        mesh=mesh,
        in_specs=(
            P(None, "dp", None, "tensor"),
            P(None, "dp", None, "tensor"),
            P(None, None, "tensor"),
            P(None, None, "tensor"),
            P(("dp", "tensor"), None),
            P("dp"),
            P("dp", None),
            P(),
        ),
        out_specs=(P(("dp", "tensor"), None), P(("dp", "tensor"), None)),
        check_vma=False,
    )
```

```python
import functools

import jax
import jax.numpy as jnp
from jax import lax
from jax.experimental import pallas as pl
from jax.experimental.pallas import tpu as pltpu
from jax.sharding import PartitionSpec as P

LAYERS = 4
SEQ = 32
WIDTH = 64
DOMAINS = 8
AXES = ("dp", "tensor")
NX, NY, NZ, NC = 4, 8, 8, 2
ORDER = ((0, 0), (0, 1), (2, 0), (1, 0), (1, 1), (3, 0), (3, 1), (2, 1))
LANES = 128
PAIRS = WIDTH * WIDTH // LANES


def flat(x, y, z, c):
    return (x * 16 + (y // 4) * 8 + z) * 8 + (y % 4) * 2 + c


def places():
    return [(x, y, z, c) for x in range(NX) for y in range(NY) for z in range(NZ) for c in range(NC)]


def partition(members):
    groups, seen = [], set()
    for place in places():
        group = [flat(*m) for m in members(*place)]
        if group[0] not in seen:
            seen.update(group)
            groups.append(group)
    return groups


def sharing_members(x, y, z, c):
    return [(i, y, (z & 6) | zl, core) for i in range(NX) for zl in range(2) for core in range(NC)]


def class_members(x, y, z, c):
    return [
        (i, (h << 2) | ((y & 3) ^ x ^ i), k, c) for i in range(NX) for h in range(2) for k in range(NZ)
    ]


def swapped(block, change):
    return lax.ppermute(block, AXES, [(flat(*change(*p)), flat(*p)) for p in places()])


def swap_x(block, step):
    return swapped(block, lambda x, y, z, c: (x ^ step, y, z, c))


def swap_z(block):
    return swapped(block, lambda x, y, z, c: (x, y, z ^ 1, c))


def swap_core(block):
    return swapped(block, lambda x, y, z, c: (x, y, z, c ^ 1))


def here():
    dp, tensor = lax.axis_index("dp"), lax.axis_index("tensor")
    return dp >> 4, tensor >> 1, dp & 1, tensor & 1


def project_kernel(
    in_ref, grad_ref, in_proj_ref, out_proj_ref, out_ref, in_buf, grad_buf, in_proj_buf, out_proj_buf, sems
):
    x, _, _, _ = here()
    sources = (in_ref, grad_ref, in_proj_ref, out_proj_ref)
    buffers = (in_buf, grad_buf, in_proj_buf, out_proj_buf)
    copies = []
    for layer in range(LAYERS):
        copies.append([
            pltpu.make_async_copy(source.at[layer], buffer.at[layer], sems.at[layer, i])
            for i, (source, buffer) in enumerate(zip(sources, buffers))
        ])
        for copy in copies[layer]:
            copy.start()

    def side(rows, proj):
        return lax.dot_general(
            rows.reshape(-1, rows.shape[-1]), proj, (((1,), (1,)), ((), ())), preferred_element_type=jnp.float32
        )

    for layer in range(LAYERS):
        for copy in copies[layer]:
            copy.wait()
        both = [side(in_buf[layer], in_proj_buf[layer]), side(grad_buf[layer], out_proj_buf[layer])]
        out_ref[pl.ds(x ^ layer, 1)] = jnp.concatenate(both, axis=1)[None]


def project(query_inputs, query_output_grads, in_projection, out_projection):
    _, queries, seq, depth = query_inputs.shape
    hbm = pl.BlockSpec(memory_space=pltpu.HBM)
    return pl.pallas_call(
        project_kernel,
        out_shape=jax.ShapeDtypeStruct((LAYERS, queries * seq, 2 * WIDTH), jnp.float32),
        in_specs=[hbm] * 4,
        out_specs=pl.BlockSpec(memory_space=pltpu.VMEM),
        scratch_shapes=[
            pltpu.VMEM(query_inputs.shape, query_inputs.dtype),
            pltpu.VMEM(query_inputs.shape, query_inputs.dtype),
            pltpu.VMEM(in_projection.shape, in_projection.dtype),
            pltpu.VMEM(in_projection.shape, in_projection.dtype),
            pltpu.SemaphoreType.DMA((LAYERS, 4)),
        ],
        compiler_params=pltpu.CompilerParams(vmem_limit_bytes=60 * 1024 * 1024),
        name="project",
    )(query_inputs, query_output_grads, in_projection, out_projection)


def outer_kernel(lengths_ref, mask_ref, parts_ref, out_ref, rows_ref, blocks_buf, sems):
    _, _, _, core = here()
    total = parts_ref[0]
    for part in range(1, parts_ref.shape[0]):
        total = total + parts_ref[part]
    row = lax.broadcasted_iota(jnp.int32, (SEQ, SEQ), 0)
    col = lax.broadcasted_iota(jnp.int32, (SEQ, SEQ), 1)
    first = lax.broadcasted_iota(jnp.int32, (SEQ, LANES), 1) < WIDTH
    inner, weighted = [], []
    for k in range(2):
        mask = jnp.where(core == 0, mask_ref[k : k + 1, :], mask_ref[2 + k : 3 + k, :])
        kept = (row == col) & (col < lengths_ref[2 * core + k])
        weight = jnp.sum(jnp.where(kept, mask, 0).astype(jnp.float32), axis=1, keepdims=True)
        factors = total[k * SEQ : (k + 1) * SEQ]
        inner.append(jnp.concatenate([factors[:, :WIDTH]] * 2, axis=1))
        weighted.append(factors[:, WIDTH:] * weight)
    members, half, _ = blocks_buf.shape[1:]
    copies = []
    for part in range(2):
        for p in range(part * half // 2, (part + 1) * half // 2):
            for k in range(2):
                low = jnp.broadcast_to(weighted[k][:, 2 * p : 2 * p + 1], (SEQ, LANES))
                high = jnp.broadcast_to(weighted[k][:, 2 * p + 1 : 2 * p + 2], (SEQ, LANES))
                product = jnp.where(first, low, high) * inner[k]
                rows_ref[2 * p + k : 2 * p + k + 1, :] = jnp.sum(product, axis=0, keepdims=True)
        block = rows_ref[part * half : (part + 1) * half, :].astype(jnp.bfloat16)
        for m in range(members):
            blocks_buf[part, m] = block
        copies.append(pltpu.make_async_copy(blocks_buf.at[part], out_ref.at[:, part], sems.at[part]))
        copies[part].start()
    for copy in copies:
        copy.wait()


def outer(lengths, loss_mask, parts, members):
    vmem = pl.BlockSpec(memory_space=pltpu.VMEM)
    blocks = pl.pallas_call(
        outer_kernel,
        out_shape=jax.ShapeDtypeStruct((members // 2, 2, PAIRS, LANES), jnp.bfloat16),
        in_specs=[pl.BlockSpec(memory_space=pltpu.SMEM), vmem, vmem],
        out_specs=pl.BlockSpec(memory_space=pltpu.HBM),
        scratch_shapes=[
            pltpu.VMEM((2 * PAIRS, LANES), jnp.float32),
            pltpu.VMEM((2, members // 2, PAIRS, LANES), jnp.bfloat16),
            pltpu.SemaphoreType.DMA((2,)),
        ],
        compiler_params=pltpu.CompilerParams(vmem_limit_bytes=16 * 1024 * 1024),
        cost_estimate=pl.CostEstimate(flops=0, bytes_accessed=60 * 1024 * 1024, transcendentals=0),
        name="outer",
    )(lengths, loss_mask, parts)
    return blocks.reshape(members, PAIRS, LANES)


def finish_kernel(parts_ref, domains_ref, scores_ref, influence_ref):
    def half(core):
        total = parts_ref[core].astype(jnp.float32)
        for part in range(core + NC, parts_ref.shape[0], NC):
            total = total + parts_ref[part].astype(jnp.float32)
        return total

    total = jnp.concatenate([half(core) for core in range(NC)], axis=1)
    queries = total.shape[1]
    column = lax.broadcasted_iota(jnp.int32, (queries, queries), 0)
    there = lax.broadcasted_iota(jnp.int32, (queries, queries), 1)
    target = ((column & 63) << 2) + ((column >> 7) << 1) + ((column >> 6) & 1)
    place = (target == there).astype(jnp.float32)
    scores = jnp.dot(total, place, precision=lax.Precision.HIGHEST, preferred_element_type=jnp.float32)
    scores_ref[...] = scores
    lane = lax.broadcasted_iota(jnp.int32, (queries, DOMAINS), 1)
    onehot = (domains_ref[...] == lane).astype(jnp.float32)
    counts = jnp.sum(onehot, axis=0, keepdims=True)
    sums = jnp.dot(scores, onehot, precision=lax.Precision.HIGHEST, preferred_element_type=jnp.float32)
    influence_ref[...] = (sums / counts).T


def finish(parts, domains):
    _, rows, half = parts.shape
    queries = NC * half
    return pl.pallas_call(
        finish_kernel,
        out_shape=(
            jax.ShapeDtypeStruct((rows, queries), jnp.float32),
            jax.ShapeDtypeStruct((DOMAINS, rows), jnp.float32),
        ),
        compiler_params=pltpu.CompilerParams(vmem_limit_bytes=16 * 1024 * 1024),
        name="finish",
    )(parts, domains)


def score_kernel(*refs):
    *rows_refs, blocks_ref, out_ref, rows_buf, queries_buf = refs
    x, _, z_low, core = here()
    lines, sources, lanes = blocks_ref.shape
    for line in range(lines):
        pair, query = line // 2, line % 2
        queries_buf[query * sources : (query + 1) * sources, pair * lanes : (pair + 1) * lanes] = blocks_ref[line]
    at = 0
    for ref in rows_refs:
        rows_buf[at : at + ref.shape[0], :] = ref[...]
        at += ref.shape[0]
    result = lax.dot_general(
        rows_buf[...], queries_buf[...], (((1,), (1,)), ((), ())), preferred_element_type=jnp.float32
    )
    rows = out_ref.shape[1]
    at = 0
    for other_core in range(NC):
        for step, other_z in ORDER:
            member = ((x ^ step) * 2 + (z_low ^ other_z)) * NC + (core ^ other_core)
            out_ref[pl.ds(member, 1)] = result[at : at + rows].astype(out_ref.dtype)[None]
            at += rows


def score(rows, blocks):
    vmem = pl.BlockSpec(memory_space=pltpu.VMEM)
    count = sum(block.shape[0] for block in rows)
    width = rows[0].shape[1]
    members = 2 * NX * NC
    queries = 2 * blocks.shape[1]
    return pl.pallas_call(
        score_kernel,
        out_shape=jax.ShapeDtypeStruct((members, count // members, queries), jnp.bfloat16),
        in_specs=[vmem] * (len(rows) + 1),
        out_specs=vmem,
        scratch_shapes=[
            pltpu.VMEM((count, width), jnp.bfloat16),
            pltpu.VMEM((queries, width), jnp.bfloat16),
        ],
        compiler_params=pltpu.CompilerParams(vmem_limit_bytes=24 * 1024 * 1024),
        name="score",
    )(*rows, blocks)


def after(block, *others):
    return lax.optimization_barrier((block,) + others)[0]


def exchange(blocks, members):
    return lax.all_to_all(blocks, AXES, 0, 0, axis_index_groups=partition(members))


def body(
    query_inputs,
    query_output_grads,
    in_projection,
    out_projection,
    train_grads,
    lengths,
    loss_mask,
    domains,
):
    x, y_lo, z_low, _ = here()
    count, ktot = train_grads.shape
    width = ktot // LAYERS // 2

    def half(which):
        return jnp.concatenate(
            [lax.dynamic_slice_in_dim(train_grads, (2 * i + which) * width, width, axis=1) for i in range(LAYERS)], axis=1
        )

    kept, other = half(z_low), swap_z(half(1 - z_low))

    def columns(step):
        at = (x ^ y_lo ^ step) * width
        return jnp.concatenate(
            [lax.dynamic_slice_in_dim(block, at, width, axis=1) for block in (kept, other)], axis=0
        )

    layer = lax.dynamic_slice_in_dim(train_grads, (x ^ y_lo ^ 2) * 2 * width, 2 * width, axis=1)
    layer = after(swap_x(layer, 2), other)
    parts = project(query_inputs, query_output_grads, in_projection, out_projection)
    parts = parts.reshape(2 * LAYERS, -1, 2 * WIDTH)
    parts = lax.all_to_all(parts, "tensor", 0, 0)

    across = [
        lax.dynamic_slice_in_dim(layer, z_low * width, width, axis=1),
        swap_z(lax.dynamic_slice_in_dim(layer, (1 - z_low) * width, width, axis=1)),
    ]

    ring = [swap_x(columns(step), step) for step in (1, 3)]
    rows = [
        jnp.concatenate([columns(0), across[0], ring[0]], axis=0),
        jnp.concatenate([ring[1], across[1]], axis=0),
    ]
    blocks = outer(lengths, loss_mask, parts, len(class_members(0, 0, 0, 0)))
    blocks = exchange(blocks, class_members)
    blocks = blocks.transpose(1, 0, 2)
    rows += [swap_core(block) for block in rows]

    parts = exchange(score(rows, blocks), sharing_members)
    scores, influence = finish(parts, domains)
    return scores, influence.T


def solution(mesh):
    return jax.shard_map(
        body,
        mesh=mesh,
        in_specs=(
            P(None, "dp", None, "tensor"),
            P(None, "dp", None, "tensor"),
            P(None, None, "tensor"),
            P(None, None, "tensor"),
            P(("dp", "tensor"), None),
            P("dp"),
            P("dp", None),
            P(),
        ),
        out_specs=(P(("dp", "tensor"), None), P(("dp", "tensor"), None)),
        check_vma=False,
    )
```

```python
import functools

import jax
import jax.numpy as jnp
from jax import lax
from jax.experimental import pallas as pl
from jax.experimental.pallas import tpu as pltpu
from jax.sharding import PartitionSpec as P

LAYERS = 4
SEQ = 32
WIDTH = 64
DOMAINS = 8
AXES = ("dp", "tensor")
NX, NY, NZ, NC = 4, 8, 8, 2
ORDER = ((0, 0), (0, 1), (2, 0), (1, 0), (1, 1), (3, 0), (3, 1), (2, 1))
LANES = 128
PAIRS = WIDTH * WIDTH // LANES


def flat(x, y, z, c):
    return (x * 16 + (y // 4) * 8 + z) * 8 + (y % 4) * 2 + c


def places():
    return [(x, y, z, c) for x in range(NX) for y in range(NY) for z in range(NZ) for c in range(NC)]


def partition(members):
    groups, seen = [], set()
    for place in places():
        group = [flat(*m) for m in members(*place)]
        if group[0] not in seen:
            seen.update(group)
            groups.append(group)
    return groups


def sharing_members(x, y, z, c):
    return [(i, y, (z & 6) | zl, core) for i in range(NX) for zl in range(2) for core in range(NC)]


def class_members(x, y, z, c):
    return [
        (i, (h << 2) | ((y & 3) ^ x ^ i), k, c) for i in range(NX) for h in range(2) for k in range(NZ)
    ]


def swapped(block, change):
    return lax.ppermute(block, AXES, [(flat(*change(*p)), flat(*p)) for p in places()])


def swap_x(block, step):
    return swapped(block, lambda x, y, z, c: (x ^ step, y, z, c))


def swap_z(block):
    return swapped(block, lambda x, y, z, c: (x, y, z ^ 1, c))


def swap_core(block):
    return swapped(block, lambda x, y, z, c: (x, y, z, c ^ 1))


def here():
    dp, tensor = lax.axis_index("dp"), lax.axis_index("tensor")
    return dp >> 4, tensor >> 1, dp & 1, tensor & 1


def project_kernel(
    in_ref, grad_ref, in_proj_ref, out_proj_ref, out_ref, in_buf, grad_buf, in_proj_buf, out_proj_buf, sems
):
    x, _, _, _ = here()
    sources = (in_ref, grad_ref, in_proj_ref, out_proj_ref)
    buffers = (in_buf, grad_buf, in_proj_buf, out_proj_buf)
    copies = []
    for layer in range(LAYERS):
        copies.append([
            pltpu.make_async_copy(source.at[layer], buffer.at[layer], sems.at[layer, i])
            for i, (source, buffer) in enumerate(zip(sources, buffers))
        ])
        for copy in copies[layer]:
            copy.start()

    def side(rows, proj):
        return lax.dot_general(
            rows.reshape(-1, rows.shape[-1]), proj, (((1,), (1,)), ((), ())), preferred_element_type=jnp.float32
        )

    for layer in range(LAYERS):
        for copy in copies[layer]:
            copy.wait()
        both = [side(in_buf[layer], in_proj_buf[layer]), side(grad_buf[layer], out_proj_buf[layer])]
        out_ref[pl.ds(x ^ layer, 1)] = jnp.concatenate(both, axis=1)[None]


def project(query_inputs, query_output_grads, in_projection, out_projection):
    _, queries, seq, depth = query_inputs.shape
    hbm = pl.BlockSpec(memory_space=pltpu.HBM)
    return pl.pallas_call(
        project_kernel,
        out_shape=jax.ShapeDtypeStruct((LAYERS, queries * seq, 2 * WIDTH), jnp.float32),
        in_specs=[hbm] * 4,
        out_specs=pl.BlockSpec(memory_space=pltpu.VMEM),
        scratch_shapes=[
            pltpu.VMEM(query_inputs.shape, query_inputs.dtype),
            pltpu.VMEM(query_inputs.shape, query_inputs.dtype),
            pltpu.VMEM(in_projection.shape, in_projection.dtype),
            pltpu.VMEM(in_projection.shape, in_projection.dtype),
            pltpu.SemaphoreType.DMA((LAYERS, 4)),
        ],
        compiler_params=pltpu.CompilerParams(vmem_limit_bytes=60 * 1024 * 1024),
        name="project",
    )(query_inputs, query_output_grads, in_projection, out_projection)


def outer_kernel(lengths_ref, mask_ref, parts_ref, out_ref, rows_ref, blocks_buf, sems):
    _, _, _, core = here()
    total = parts_ref[0]
    for part in range(1, parts_ref.shape[0]):
        total = total + parts_ref[part]
    row = lax.broadcasted_iota(jnp.int32, (SEQ, SEQ), 0)
    col = lax.broadcasted_iota(jnp.int32, (SEQ, SEQ), 1)
    first = lax.broadcasted_iota(jnp.int32, (SEQ, LANES), 1) < WIDTH
    inner, weighted = [], []
    for k in range(2):
        mask = jnp.where(core == 0, mask_ref[k : k + 1, :], mask_ref[2 + k : 3 + k, :])
        kept = (row == col) & (col < lengths_ref[2 * core + k])
        weight = jnp.sum(jnp.where(kept, mask, 0).astype(jnp.float32), axis=1, keepdims=True)
        factors = total[k * SEQ : (k + 1) * SEQ]
        inner.append(jnp.concatenate([factors[:, :WIDTH]] * 2, axis=1))
        weighted.append(factors[:, WIDTH:] * weight)
    members, half, _ = blocks_buf.shape[1:]
    copies = []
    for part in range(2):
        for p in range(part * half // 2, (part + 1) * half // 2):
            for k in range(2):
                low = jnp.broadcast_to(weighted[k][:, 2 * p : 2 * p + 1], (SEQ, LANES))
                high = jnp.broadcast_to(weighted[k][:, 2 * p + 1 : 2 * p + 2], (SEQ, LANES))
                product = jnp.where(first, low, high) * inner[k]
                rows_ref[2 * p + k : 2 * p + k + 1, :] = jnp.sum(product, axis=0, keepdims=True)
        block = rows_ref[part * half : (part + 1) * half, :].astype(jnp.bfloat16)
        for m in range(members):
            blocks_buf[part, m] = block
        copies.append(pltpu.make_async_copy(blocks_buf.at[part], out_ref.at[:, part], sems.at[part]))
        copies[part].start()
    for copy in copies:
        copy.wait()


def outer(lengths, loss_mask, parts, members):
    vmem = pl.BlockSpec(memory_space=pltpu.VMEM)
    blocks = pl.pallas_call(
        outer_kernel,
        out_shape=jax.ShapeDtypeStruct((members // 2, 2, PAIRS, LANES), jnp.bfloat16),
        in_specs=[pl.BlockSpec(memory_space=pltpu.SMEM), vmem, vmem],
        out_specs=pl.BlockSpec(memory_space=pltpu.HBM),
        scratch_shapes=[
            pltpu.VMEM((2 * PAIRS, LANES), jnp.float32),
            pltpu.VMEM((2, members // 2, PAIRS, LANES), jnp.bfloat16),
            pltpu.SemaphoreType.DMA((2,)),
        ],
        compiler_params=pltpu.CompilerParams(vmem_limit_bytes=16 * 1024 * 1024),
        cost_estimate=pl.CostEstimate(flops=0, bytes_accessed=60 * 1024 * 1024, transcendentals=0),
        name="outer",
    )(lengths, loss_mask, parts)
    return blocks.reshape(members, PAIRS, LANES)


def finish_kernel(parts_ref, domains_ref, scores_ref, influence_ref):
    def half(core):
        total = parts_ref[core].astype(jnp.float32)
        for part in range(core + NC, parts_ref.shape[0], NC):
            total = total + parts_ref[part].astype(jnp.float32)
        return total

    total = jnp.concatenate([half(core) for core in range(NC)], axis=1)
    queries = total.shape[1]
    column = lax.broadcasted_iota(jnp.int32, (queries, queries), 0)
    there = lax.broadcasted_iota(jnp.int32, (queries, queries), 1)
    target = ((column & 63) << 2) + ((column >> 7) << 1) + ((column >> 6) & 1)
    place = (target == there).astype(jnp.float32)
    scores = jnp.dot(total, place, precision=lax.Precision.HIGHEST, preferred_element_type=jnp.float32)
    scores_ref[...] = scores
    onehot = (domains_ref[...] == lax.broadcasted_iota(jnp.int32, (DOMAINS, queries), 0)).astype(jnp.float32)
    counts = jnp.sum(onehot, axis=1, keepdims=True)
    sums = lax.dot_general(
        onehot,
        scores,
        (((1,), (1,)), ((), ())),
        precision=lax.Precision.HIGHEST,
        preferred_element_type=jnp.float32,
    )
    influence_ref[...] = sums / counts


def finish(parts, domains):
    _, rows, half = parts.shape
    queries = NC * half
    return pl.pallas_call(
        finish_kernel,
        out_shape=(
            jax.ShapeDtypeStruct((rows, queries), jnp.float32),
            jax.ShapeDtypeStruct((DOMAINS, rows), jnp.float32),
        ),
        compiler_params=pltpu.CompilerParams(vmem_limit_bytes=16 * 1024 * 1024),
        name="finish",
    )(parts, domains.reshape(1, queries))


def score_kernel(*refs):
    *rows_refs, blocks_ref, out_ref, rows_buf, queries_buf = refs
    x, _, z_low, core = here()
    lines, sources, lanes = blocks_ref.shape
    for line in range(lines):
        pair, query = line // 2, line % 2
        queries_buf[query * sources : (query + 1) * sources, pair * lanes : (pair + 1) * lanes] = blocks_ref[line]
    at = 0
    for ref in rows_refs:
        rows_buf[at : at + ref.shape[0], :] = ref[...]
        at += ref.shape[0]
    result = lax.dot_general(
        rows_buf[...], queries_buf[...], (((1,), (1,)), ((), ())), preferred_element_type=jnp.float32
    )
    rows = out_ref.shape[1]
    at = 0
    for other_core in range(NC):
        for step, other_z in ORDER:
            member = ((x ^ step) * 2 + (z_low ^ other_z)) * NC + (core ^ other_core)
            out_ref[pl.ds(member, 1)] = result[at : at + rows].astype(out_ref.dtype)[None]
            at += rows


def score(rows, blocks):
    vmem = pl.BlockSpec(memory_space=pltpu.VMEM)
    count = sum(block.shape[0] for block in rows)
    width = rows[0].shape[1]
    members = 2 * NX * NC
    queries = 2 * blocks.shape[1]
    return pl.pallas_call(
        score_kernel,
        out_shape=jax.ShapeDtypeStruct((members, count // members, queries), jnp.bfloat16),
        in_specs=[vmem] * (len(rows) + 1),
        out_specs=vmem,
        scratch_shapes=[
            pltpu.VMEM((count, width), jnp.bfloat16),
            pltpu.VMEM((queries, width), jnp.bfloat16),
        ],
        compiler_params=pltpu.CompilerParams(vmem_limit_bytes=24 * 1024 * 1024),
        name="score",
    )(*rows, blocks)


def after(block, *others):
    return lax.optimization_barrier((block,) + others)[0]


def exchange(blocks, members):
    return lax.all_to_all(blocks, AXES, 0, 0, axis_index_groups=partition(members))


def body(
    query_inputs,
    query_output_grads,
    in_projection,
    out_projection,
    train_grads,
    lengths,
    loss_mask,
    domains,
):
    x, y_lo, z_low, _ = here()
    count, ktot = train_grads.shape
    width = ktot // LAYERS // 2

    def half(which):
        return jnp.concatenate(
            [lax.dynamic_slice_in_dim(train_grads, (2 * i + which) * width, width, axis=1) for i in range(LAYERS)], axis=1
        )

    kept, other = half(z_low), swap_z(half(1 - z_low))

    def columns(step):
        at = (x ^ y_lo ^ step) * width
        return jnp.concatenate(
            [lax.dynamic_slice_in_dim(block, at, width, axis=1) for block in (kept, other)], axis=0
        )

    layer = lax.dynamic_slice_in_dim(train_grads, (x ^ y_lo ^ 2) * 2 * width, 2 * width, axis=1)
    layer = after(swap_x(layer, 2), other)
    parts = project(query_inputs, query_output_grads, in_projection, out_projection)
    parts = parts.reshape(2 * LAYERS, -1, 2 * WIDTH)
    parts = lax.all_to_all(parts, "tensor", 0, 0)

    across = [
        lax.dynamic_slice_in_dim(layer, z_low * width, width, axis=1),
        swap_z(lax.dynamic_slice_in_dim(layer, (1 - z_low) * width, width, axis=1)),
    ]

    ring = [swap_x(columns(step), step) for step in (1, 3)]
    rows = [
        jnp.concatenate([columns(0), across[0], ring[0]], axis=0),
        jnp.concatenate([ring[1], across[1]], axis=0),
    ]
    blocks = outer(lengths, loss_mask, parts, len(class_members(0, 0, 0, 0)))
    blocks = exchange(blocks, class_members)
    blocks = blocks.transpose(1, 0, 2)
    rows += [swap_core(block) for block in rows]

    parts = exchange(score(rows, blocks), sharing_members)
    scores, influence = finish(parts, domains)
    return scores, influence.T


def solution(mesh):
    return jax.shard_map(
        body,
        mesh=mesh,
        in_specs=(
            P(None, "dp", None, "tensor"),
            P(None, "dp", None, "tensor"),
            P(None, None, "tensor"),
            P(None, None, "tensor"),
            P(("dp", "tensor"), None),
            P("dp"),
            P("dp", None),
            P(),
        ),
        out_specs=(P(("dp", "tensor"), None), P(("dp", "tensor"), None)),
        check_vma=False,
    )
```

```python
import functools

import jax
import jax.numpy as jnp
from jax import lax
from jax.experimental import pallas as pl
from jax.experimental.pallas import tpu as pltpu
from jax.sharding import PartitionSpec as P

LAYERS = 4
SEQ = 32
WIDTH = 64
DOMAINS = 8
AXES = ("dp", "tensor")
NX, NY, NZ, NC = 4, 8, 8, 2
ORDER = ((0, 0), (0, 1), (2, 0), (1, 0), (1, 1), (3, 0), (3, 1), (2, 1))
LANES = 128
PAIRS = WIDTH * WIDTH // LANES


def flat(x, y, z, c):
    return (x * 16 + (y // 4) * 8 + z) * 8 + (y % 4) * 2 + c


def places():
    return [(x, y, z, c) for x in range(NX) for y in range(NY) for z in range(NZ) for c in range(NC)]


def partition(members):
    groups, seen = [], set()
    for place in places():
        group = [flat(*m) for m in members(*place)]
        if group[0] not in seen:
            seen.update(group)
            groups.append(group)
    return groups


def sharing_members(x, y, z, c):
    return [(i, y, (z & 6) | zl, core) for i in range(NX) for zl in range(2) for core in range(NC)]


def class_members(x, y, z, c):
    return [
        (i, (h << 2) | ((y & 3) ^ x ^ i), k, c) for i in range(NX) for h in range(2) for k in range(NZ)
    ]


def swapped(block, change):
    return lax.ppermute(block, AXES, [(flat(*change(*p)), flat(*p)) for p in places()])


def swap_x(block, step):
    return swapped(block, lambda x, y, z, c: (x ^ step, y, z, c))


def swap_z(block):
    return swapped(block, lambda x, y, z, c: (x, y, z ^ 1, c))


def swap_core(block):
    return swapped(block, lambda x, y, z, c: (x, y, z, c ^ 1))


def here():
    dp, tensor = lax.axis_index("dp"), lax.axis_index("tensor")
    return dp >> 4, tensor >> 1, dp & 1, tensor & 1


def project_kernel(
    in_ref, grad_ref, in_proj_ref, out_proj_ref, out_ref, in_buf, grad_buf, in_proj_buf, out_proj_buf, out_buf, sems, out_sems
):
    x, _, _, _ = here()
    sources = (in_ref, grad_ref, in_proj_ref, out_proj_ref)
    buffers = (in_buf, grad_buf, in_proj_buf, out_proj_buf)
    copies = []
    for layer in range(LAYERS):
        copies.append([
            pltpu.make_async_copy(source.at[layer], buffer.at[layer], sems.at[layer, i])
            for i, (source, buffer) in enumerate(zip(sources, buffers))
        ])
        for copy in copies[layer]:
            copy.start()

    def side(rows, proj):
        return lax.dot_general(
            rows.reshape(-1, rows.shape[-1]), proj, (((1,), (1,)), ((), ())), preferred_element_type=jnp.float32
        )

    stores = []
    for layer in range(LAYERS):
        for copy in copies[layer]:
            copy.wait()
        both = [side(in_buf[layer], in_proj_buf[layer]), side(grad_buf[layer], out_proj_buf[layer])]
        out_buf[layer] = jnp.concatenate(both, axis=1)
        stores.append(pltpu.make_async_copy(out_buf.at[layer], out_ref.at[x ^ layer], out_sems.at[layer]))
        stores[layer].start()
    for store in stores:
        store.wait()


def project(query_inputs, query_output_grads, in_projection, out_projection):
    _, queries, seq, depth = query_inputs.shape
    hbm = pl.BlockSpec(memory_space=pltpu.HBM)
    return pl.pallas_call(
        project_kernel,
        out_shape=jax.ShapeDtypeStruct((LAYERS, queries * seq, 2 * WIDTH), jnp.float32),
        in_specs=[hbm] * 4,
        out_specs=hbm,
        scratch_shapes=[
            pltpu.VMEM(query_inputs.shape, query_inputs.dtype),
            pltpu.VMEM(query_inputs.shape, query_inputs.dtype),
            pltpu.VMEM(in_projection.shape, in_projection.dtype),
            pltpu.VMEM(in_projection.shape, in_projection.dtype),
            pltpu.VMEM((LAYERS, queries * seq, 2 * WIDTH), jnp.float32),
            pltpu.SemaphoreType.DMA((LAYERS, 4)),
            pltpu.SemaphoreType.DMA((LAYERS,)),
        ],
        compiler_params=pltpu.CompilerParams(vmem_limit_bytes=60 * 1024 * 1024),
        name="project",
    )(query_inputs, query_output_grads, in_projection, out_projection)


def outer_kernel(lengths_ref, mask_ref, parts_ref, out_ref, rows_ref, blocks_buf, sems):
    _, _, _, core = here()
    total = parts_ref[0]
    for part in range(1, parts_ref.shape[0]):
        total = total + parts_ref[part]
    row = lax.broadcasted_iota(jnp.int32, (SEQ, SEQ), 0)
    col = lax.broadcasted_iota(jnp.int32, (SEQ, SEQ), 1)
    first = lax.broadcasted_iota(jnp.int32, (SEQ, LANES), 1) < WIDTH
    inner, weighted = [], []
    for k in range(2):
        mask = jnp.where(core == 0, mask_ref[k : k + 1, :], mask_ref[2 + k : 3 + k, :])
        kept = (row == col) & (col < lengths_ref[2 * core + k])
        weight = jnp.sum(jnp.where(kept, mask, 0).astype(jnp.float32), axis=1, keepdims=True)
        factors = total[k * SEQ : (k + 1) * SEQ]
        inner.append(jnp.concatenate([factors[:, :WIDTH]] * 2, axis=1))
        weighted.append(factors[:, WIDTH:] * weight)
    members, half, _ = blocks_buf.shape[1:]
    copies = []
    for part in range(2):
        for p in range(part * half // 2, (part + 1) * half // 2):
            for k in range(2):
                low = jnp.broadcast_to(weighted[k][:, 2 * p : 2 * p + 1], (SEQ, LANES))
                high = jnp.broadcast_to(weighted[k][:, 2 * p + 1 : 2 * p + 2], (SEQ, LANES))
                product = jnp.where(first, low, high) * inner[k]
                rows_ref[2 * p + k : 2 * p + k + 1, :] = jnp.sum(product, axis=0, keepdims=True)
        block = rows_ref[part * half : (part + 1) * half, :].astype(jnp.bfloat16)
        for m in range(members):
            blocks_buf[part, m] = block
        copies.append(pltpu.make_async_copy(blocks_buf.at[part], out_ref.at[:, part], sems.at[part]))
        copies[part].start()
    for copy in copies:
        copy.wait()


def outer(lengths, loss_mask, parts, members):
    vmem = pl.BlockSpec(memory_space=pltpu.VMEM)
    blocks = pl.pallas_call(
        outer_kernel,
        out_shape=jax.ShapeDtypeStruct((members // 2, 2, PAIRS, LANES), jnp.bfloat16),
        in_specs=[pl.BlockSpec(memory_space=pltpu.SMEM), vmem, vmem],
        out_specs=pl.BlockSpec(memory_space=pltpu.HBM),
        scratch_shapes=[
            pltpu.VMEM((2 * PAIRS, LANES), jnp.float32),
            pltpu.VMEM((2, members // 2, PAIRS, LANES), jnp.bfloat16),
            pltpu.SemaphoreType.DMA((2,)),
        ],
        compiler_params=pltpu.CompilerParams(vmem_limit_bytes=16 * 1024 * 1024),
        cost_estimate=pl.CostEstimate(flops=0, bytes_accessed=60 * 1024 * 1024, transcendentals=0),
        name="outer",
    )(lengths, loss_mask, parts)
    return blocks.reshape(members, PAIRS, LANES)


def finish_kernel(parts_ref, domains_ref, scores_ref, influence_ref):
    def half(core):
        total = parts_ref[core].astype(jnp.float32)
        for part in range(core + NC, parts_ref.shape[0], NC):
            total = total + parts_ref[part].astype(jnp.float32)
        return total

    total = jnp.concatenate([half(core) for core in range(NC)], axis=1)
    queries = total.shape[1]
    column = lax.broadcasted_iota(jnp.int32, (queries, queries), 0)
    there = lax.broadcasted_iota(jnp.int32, (queries, queries), 1)
    target = ((column & 63) << 2) + ((column >> 7) << 1) + ((column >> 6) & 1)
    place = (target == there).astype(jnp.float32)
    scores = jnp.dot(total, place, precision=lax.Precision.HIGHEST, preferred_element_type=jnp.float32)
    scores_ref[...] = scores
    onehot = (domains_ref[...] == lax.broadcasted_iota(jnp.int32, (DOMAINS, queries), 0)).astype(jnp.float32)
    counts = jnp.sum(onehot, axis=1, keepdims=True)
    sums = lax.dot_general(
        onehot,
        scores,
        (((1,), (1,)), ((), ())),
        precision=lax.Precision.HIGHEST,
        preferred_element_type=jnp.float32,
    )
    influence_ref[...] = sums / counts


def finish(parts, domains):
    _, rows, half = parts.shape
    queries = NC * half
    return pl.pallas_call(
        finish_kernel,
        out_shape=(
            jax.ShapeDtypeStruct((rows, queries), jnp.float32),
            jax.ShapeDtypeStruct((DOMAINS, rows), jnp.float32),
        ),
        compiler_params=pltpu.CompilerParams(vmem_limit_bytes=16 * 1024 * 1024),
        name="finish",
    )(parts, domains.reshape(1, queries))


def score_kernel(*refs):
    *rows_refs, blocks_ref, out_ref, rows_buf, queries_buf = refs
    x, _, z_low, core = here()
    lines, sources, lanes = blocks_ref.shape
    for line in range(lines):
        pair, query = line // 2, line % 2
        queries_buf[query * sources : (query + 1) * sources, pair * lanes : (pair + 1) * lanes] = blocks_ref[line]
    at = 0
    for ref in rows_refs:
        rows_buf[at : at + ref.shape[0], :] = ref[...]
        at += ref.shape[0]
    result = lax.dot_general(
        rows_buf[...], queries_buf[...], (((1,), (1,)), ((), ())), preferred_element_type=jnp.float32
    )
    rows = out_ref.shape[1]
    at = 0
    for other_core in range(NC):
        for step, other_z in ORDER:
            member = ((x ^ step) * 2 + (z_low ^ other_z)) * NC + (core ^ other_core)
            out_ref[pl.ds(member, 1)] = result[at : at + rows].astype(out_ref.dtype)[None]
            at += rows


def score(rows, blocks):
    vmem = pl.BlockSpec(memory_space=pltpu.VMEM)
    count = sum(block.shape[0] for block in rows)
    width = rows[0].shape[1]
    members = 2 * NX * NC
    queries = 2 * blocks.shape[1]
    return pl.pallas_call(
        score_kernel,
        out_shape=jax.ShapeDtypeStruct((members, count // members, queries), jnp.bfloat16),
        in_specs=[vmem] * (len(rows) + 1),
        out_specs=vmem,
        scratch_shapes=[
            pltpu.VMEM((count, width), jnp.bfloat16),
            pltpu.VMEM((queries, width), jnp.bfloat16),
        ],
        compiler_params=pltpu.CompilerParams(vmem_limit_bytes=24 * 1024 * 1024),
        name="score",
    )(*rows, blocks)


def after(block, *others):
    return lax.optimization_barrier((block,) + others)[0]


def exchange(blocks, members):
    return lax.all_to_all(blocks, AXES, 0, 0, axis_index_groups=partition(members))


def body(
    query_inputs,
    query_output_grads,
    in_projection,
    out_projection,
    train_grads,
    lengths,
    loss_mask,
    domains,
):
    x, y_lo, z_low, _ = here()
    count, ktot = train_grads.shape
    width = ktot // LAYERS // 2

    def half(which):
        return jnp.concatenate(
            [lax.dynamic_slice_in_dim(train_grads, (2 * i + which) * width, width, axis=1) for i in range(LAYERS)], axis=1
        )

    kept, other = half(z_low), swap_z(half(1 - z_low))

    def columns(step):
        at = (x ^ y_lo ^ step) * width
        return jnp.concatenate(
            [lax.dynamic_slice_in_dim(block, at, width, axis=1) for block in (kept, other)], axis=0
        )

    layer = lax.dynamic_slice_in_dim(train_grads, (x ^ y_lo ^ 2) * 2 * width, 2 * width, axis=1)
    layer = after(swap_x(layer, 2), other)
    parts = project(query_inputs, query_output_grads, in_projection, out_projection)
    parts = parts.reshape(2 * LAYERS, -1, 2 * WIDTH)
    parts = lax.all_to_all(parts, "tensor", 0, 0)

    across = [
        lax.dynamic_slice_in_dim(layer, z_low * width, width, axis=1),
        swap_z(lax.dynamic_slice_in_dim(layer, (1 - z_low) * width, width, axis=1)),
    ]

    ring = [swap_x(columns(step), step) for step in (1, 3)]
    rows = [
        jnp.concatenate([columns(0), across[0], ring[0]], axis=0),
        jnp.concatenate([ring[1], across[1]], axis=0),
    ]
    blocks = outer(lengths, loss_mask, parts, len(class_members(0, 0, 0, 0)))
    blocks = exchange(blocks, class_members)
    blocks = blocks.transpose(1, 0, 2)
    rows += [swap_core(block) for block in rows]

    parts = exchange(score(rows, blocks), sharing_members)
    scores, influence = finish(parts, domains)
    return scores, influence.T


def solution(mesh):
    return jax.shard_map(
        body,
        mesh=mesh,
        in_specs=(
            P(None, "dp", None, "tensor"),
            P(None, "dp", None, "tensor"),
            P(None, None, "tensor"),
            P(None, None, "tensor"),
            P(("dp", "tensor"), None),
            P("dp"),
            P("dp", None),
            P(),
        ),
        out_specs=(P(("dp", "tensor"), None), P(("dp", "tensor"), None)),
        check_vma=False,
    )
```

```python
import functools

import jax
import jax.numpy as jnp
from jax import lax
from jax.experimental import pallas as pl
from jax.experimental.pallas import tpu as pltpu
from jax.sharding import PartitionSpec as P

LAYERS = 4
SEQ = 32
WIDTH = 64
DOMAINS = 8
AXES = ("dp", "tensor")
NX, NY, NZ, NC = 4, 8, 8, 2
ORDER = ((0, 0), (0, 1), (2, 0), (1, 0), (1, 1), (3, 0), (3, 1), (2, 1))
LANES = 128
PAIRS = WIDTH * WIDTH // LANES


def flat(x, y, z, c):
    return (x * 16 + (y // 4) * 8 + z) * 8 + (y % 4) * 2 + c


def places():
    return [(x, y, z, c) for x in range(NX) for y in range(NY) for z in range(NZ) for c in range(NC)]


def partition(members):
    groups, seen = [], set()
    for place in places():
        group = [flat(*m) for m in members(*place)]
        if group[0] not in seen:
            seen.update(group)
            groups.append(group)
    return groups


def sharing_members(x, y, z, c):
    return [(i, y, (z & 6) | zl, core) for i in range(NX) for zl in range(2) for core in range(NC)]


def class_members(x, y, z, c):
    return [
        (i, (h << 2) | ((y & 3) ^ x ^ i), k, c) for i in range(NX) for h in range(2) for k in range(NZ)
    ]


def swapped(block, change):
    return lax.ppermute(block, AXES, [(flat(*change(*p)), flat(*p)) for p in places()])


def swap_x(block, step):
    return swapped(block, lambda x, y, z, c: (x ^ step, y, z, c))


def swap_z(block):
    return swapped(block, lambda x, y, z, c: (x, y, z ^ 1, c))


def swap_core(block):
    return swapped(block, lambda x, y, z, c: (x, y, z, c ^ 1))


def here():
    dp, tensor = lax.axis_index("dp"), lax.axis_index("tensor")
    return dp >> 4, tensor >> 1, dp & 1, tensor & 1


def project_kernel(
    in_ref, grad_ref, in_proj_ref, out_proj_ref, out_ref, in_buf, grad_buf, in_proj_buf, out_proj_buf, sems
):
    x, _, _, _ = here()
    sources = (in_ref, grad_ref, in_proj_ref, out_proj_ref)
    buffers = (in_buf, grad_buf, in_proj_buf, out_proj_buf)
    copies = []
    for layer in range(LAYERS):
        copies.append([
            pltpu.make_async_copy(source.at[layer], buffer.at[layer], sems.at[layer, i])
            for i, (source, buffer) in enumerate(zip(sources, buffers))
        ])
        for copy in copies[layer]:
            copy.start()

    def side(rows, proj):
        return lax.dot_general(
            rows.reshape(-1, rows.shape[-1]), proj, (((1,), (1,)), ((), ())), preferred_element_type=jnp.float32
        )

    for layer in range(LAYERS):
        for copy in copies[layer]:
            copy.wait()
        both = [side(in_buf[layer], in_proj_buf[layer]), side(grad_buf[layer], out_proj_buf[layer])]
        out_ref[pl.ds(x ^ layer, 1)] = jnp.concatenate(both, axis=1)[None]


def project(query_inputs, query_output_grads, in_projection, out_projection):
    _, queries, seq, depth = query_inputs.shape
    hbm = pl.BlockSpec(memory_space=pltpu.HBM)
    return pl.pallas_call(
        project_kernel,
        out_shape=jax.ShapeDtypeStruct((LAYERS, queries * seq, 2 * WIDTH), jnp.float32),
        in_specs=[hbm] * 4,
        out_specs=pl.BlockSpec(memory_space=pltpu.VMEM),
        scratch_shapes=[
            pltpu.VMEM(query_inputs.shape, query_inputs.dtype),
            pltpu.VMEM(query_inputs.shape, query_inputs.dtype),
            pltpu.VMEM(in_projection.shape, in_projection.dtype),
            pltpu.VMEM(in_projection.shape, in_projection.dtype),
            pltpu.SemaphoreType.DMA((LAYERS, 4)),
        ],
        compiler_params=pltpu.CompilerParams(vmem_limit_bytes=60 * 1024 * 1024),
        name="project",
    )(query_inputs, query_output_grads, in_projection, out_projection)


def outer_kernel(lengths_ref, mask_ref, parts_ref, out_ref, rows_ref, blocks_buf, sems):
    _, _, _, core = here()
    total = parts_ref[0]
    for part in range(1, parts_ref.shape[0]):
        total = total + parts_ref[part]
    row = lax.broadcasted_iota(jnp.int32, (SEQ, SEQ), 0)
    col = lax.broadcasted_iota(jnp.int32, (SEQ, SEQ), 1)
    first = lax.broadcasted_iota(jnp.int32, (SEQ, LANES), 1) < WIDTH
    inner, weighted = [], []
    for k in range(2):
        mask = jnp.where(core == 0, mask_ref[k : k + 1, :], mask_ref[2 + k : 3 + k, :])
        kept = (row == col) & (col < lengths_ref[2 * core + k])
        weight = jnp.sum(jnp.where(kept, mask, 0).astype(jnp.float32), axis=1, keepdims=True)
        factors = total[k * SEQ : (k + 1) * SEQ]
        inner.append(jnp.concatenate([factors[:, :WIDTH]] * 2, axis=1))
        weighted.append(factors[:, WIDTH:] * weight)
    members, half, _ = blocks_buf.shape[1:]
    copies = []
    for part in range(2):
        for p in range(part * half // 2, (part + 1) * half // 2):
            for k in range(2):
                low = jnp.broadcast_to(weighted[k][:, 2 * p : 2 * p + 1], (SEQ, LANES))
                high = jnp.broadcast_to(weighted[k][:, 2 * p + 1 : 2 * p + 2], (SEQ, LANES))
                product = jnp.where(first, low, high) * inner[k]
                rows_ref[2 * p + k : 2 * p + k + 1, :] = jnp.sum(product, axis=0, keepdims=True)
        block = rows_ref[part * half : (part + 1) * half, :].astype(jnp.bfloat16)
        for m in range(members):
            blocks_buf[part, m] = block
        copies.append(pltpu.make_async_copy(blocks_buf.at[part], out_ref.at[:, part], sems.at[part]))
        copies[part].start()
    for copy in copies:
        copy.wait()


def outer(lengths, loss_mask, parts, members):
    vmem = pl.BlockSpec(memory_space=pltpu.VMEM)
    blocks = pl.pallas_call(
        outer_kernel,
        out_shape=jax.ShapeDtypeStruct((members // 2, 2, PAIRS, LANES), jnp.bfloat16),
        in_specs=[pl.BlockSpec(memory_space=pltpu.SMEM), vmem, vmem],
        out_specs=pl.BlockSpec(memory_space=pltpu.HBM),
        scratch_shapes=[
            pltpu.VMEM((2 * PAIRS, LANES), jnp.float32),
            pltpu.VMEM((2, members // 2, PAIRS, LANES), jnp.bfloat16),
            pltpu.SemaphoreType.DMA((2,)),
        ],
        compiler_params=pltpu.CompilerParams(vmem_limit_bytes=16 * 1024 * 1024),
        cost_estimate=pl.CostEstimate(flops=0, bytes_accessed=60 * 1024 * 1024, transcendentals=0),
        name="outer",
    )(lengths, loss_mask, parts)
    return blocks.reshape(members, PAIRS, LANES)


def finish_kernel(parts_ref, domains_ref, scores_ref, influence_ref):
    def half(core):
        total = parts_ref[core].astype(jnp.float32)
        for part in range(core + NC, parts_ref.shape[0], NC):
            total = total + parts_ref[part].astype(jnp.float32)
        return total

    total = jnp.concatenate([half(core) for core in range(NC)], axis=1)
    queries = total.shape[1]
    column = lax.broadcasted_iota(jnp.int32, (queries, queries), 0)
    there = lax.broadcasted_iota(jnp.int32, (queries, queries), 1)
    target = ((column & 63) << 2) + ((column >> 7) << 1) + ((column >> 6) & 1)
    place = (target == there).astype(jnp.float32)
    scores = jnp.dot(total, place, precision=lax.Precision.HIGHEST, preferred_element_type=jnp.float32)
    scores_ref[...] = scores
    onehot = (domains_ref[...] == lax.broadcasted_iota(jnp.int32, (DOMAINS, queries), 0)).astype(jnp.float32)
    counts = jnp.sum(onehot, axis=1, keepdims=True)
    sums = lax.dot_general(
        onehot,
        scores,
        (((1,), (1,)), ((), ())),
        precision=lax.Precision.HIGHEST,
        preferred_element_type=jnp.float32,
    )
    influence_ref[...] = sums / counts


def finish(parts, domains):
    _, rows, half = parts.shape
    queries = NC * half
    return pl.pallas_call(
        finish_kernel,
        out_shape=(
            jax.ShapeDtypeStruct((rows, queries), jnp.float32),
            jax.ShapeDtypeStruct((DOMAINS, rows), jnp.float32),
        ),
        compiler_params=pltpu.CompilerParams(vmem_limit_bytes=16 * 1024 * 1024),
        name="finish",
    )(parts, domains.reshape(1, queries))


def score_kernel(*refs):
    *rows_refs, blocks_ref, out_ref, queries_buf = refs
    x, _, z_low, core = here()
    lines, sources, lanes = blocks_ref.shape
    for line in range(lines):
        pair, query = line // 2, line % 2
        queries_buf[query * sources : (query + 1) * sources, pair * lanes : (pair + 1) * lanes] = blocks_ref[line]
    places = [(other_core, *place) for other_core in range(NC) for place in ORDER]
    rows = out_ref.shape[1]
    for ref in rows_refs:
        result = lax.dot_general(
            ref[...], queries_buf[...], (((1,), (1,)), ((), ())), preferred_element_type=jnp.float32
        )
        for n in range(ref.shape[0] // rows):
            other_core, step, other_z = places.pop(0)
            member = ((x ^ step) * 2 + (z_low ^ other_z)) * NC + (core ^ other_core)
            out_ref[pl.ds(member, 1)] = result[n * rows : (n + 1) * rows].astype(out_ref.dtype)[None]


def score(rows, blocks):
    vmem = pl.BlockSpec(memory_space=pltpu.VMEM)
    count = sum(block.shape[0] for block in rows)
    width = rows[0].shape[1]
    members = 2 * NX * NC
    queries = 2 * blocks.shape[1]
    return pl.pallas_call(
        score_kernel,
        out_shape=jax.ShapeDtypeStruct((members, count // members, queries), jnp.bfloat16),
        in_specs=[vmem] * (len(rows) + 1),
        out_specs=vmem,
        scratch_shapes=[
            pltpu.VMEM((queries, width), jnp.bfloat16),
        ],
        compiler_params=pltpu.CompilerParams(vmem_limit_bytes=24 * 1024 * 1024),
        name="score",
    )(*rows, blocks)


def after(block, *others):
    return lax.optimization_barrier((block,) + others)[0]


def exchange(blocks, members):
    return lax.all_to_all(blocks, AXES, 0, 0, axis_index_groups=partition(members))


def body(
    query_inputs,
    query_output_grads,
    in_projection,
    out_projection,
    train_grads,
    lengths,
    loss_mask,
    domains,
):
    x, y_lo, z_low, _ = here()
    count, ktot = train_grads.shape
    width = ktot // LAYERS // 2

    def half(which):
        return jnp.concatenate(
            [lax.dynamic_slice_in_dim(train_grads, (2 * i + which) * width, width, axis=1) for i in range(LAYERS)], axis=1
        )

    kept, other = half(z_low), swap_z(half(1 - z_low))

    def columns(step):
        at = (x ^ y_lo ^ step) * width
        return jnp.concatenate(
            [lax.dynamic_slice_in_dim(block, at, width, axis=1) for block in (kept, other)], axis=0
        )

    layer = lax.dynamic_slice_in_dim(train_grads, (x ^ y_lo ^ 2) * 2 * width, 2 * width, axis=1)
    layer = after(swap_x(layer, 2), other)
    parts = project(query_inputs, query_output_grads, in_projection, out_projection)
    parts = parts.reshape(2 * LAYERS, -1, 2 * WIDTH)
    parts = lax.all_to_all(parts, "tensor", 0, 0)

    across = [
        lax.dynamic_slice_in_dim(layer, z_low * width, width, axis=1),
        swap_z(lax.dynamic_slice_in_dim(layer, (1 - z_low) * width, width, axis=1)),
    ]

    ring = [swap_x(columns(step), step) for step in (1, 3)]
    rows = [
        jnp.concatenate([columns(0), across[0], ring[0]], axis=0),
        jnp.concatenate([ring[1], across[1]], axis=0),
    ]
    blocks = outer(lengths, loss_mask, parts, len(class_members(0, 0, 0, 0)))
    blocks = exchange(blocks, class_members)
    blocks = blocks.transpose(1, 0, 2)
    rows += [swap_core(block) for block in rows]

    parts = exchange(score(rows, blocks), sharing_members)
    scores, influence = finish(parts, domains)
    return scores, influence.T


def solution(mesh):
    return jax.shard_map(
        body,
        mesh=mesh,
        in_specs=(
            P(None, "dp", None, "tensor"),
            P(None, "dp", None, "tensor"),
            P(None, None, "tensor"),
            P(None, None, "tensor"),
            P(("dp", "tensor"), None),
            P("dp"),
            P("dp", None),
            P(),
        ),
        out_specs=(P(("dp", "tensor"), None), P(("dp", "tensor"), None)),
        check_vma=False,
    )
```
